128 devices in a mesh: tx: 4 (over z), ty: 32 (over y, x, core).
Axes of the slice: x: 4, y: 4, z: 4, core: 2. Of those that a mesh axis runs over, the one named last changes fastest.
Arguments:
- hidden_in: bfloat16 [512, 8192], P(None, ('ty', 'tx'))
- norm_gain: bfloat16 [8192], P(('ty', 'tx')), may hold values from 0.5 to 1.5
- qkv_weight: bfloat16 [8192, 10240], P('ty', 'tx'), may hold values from -0.0625 to 0.0625
- qkv_bias: bfloat16 [10240], replicated, may hold values from -4 to 4
- key_cache: bfloat16 [512, 128, 1024], P(('ty', 'tx')), may hold values from -6 to 6
- value_cache: bfloat16 [512, 128, 1024], P(('ty', 'tx')), may hold values from -6 to 6
- lengths: int32 [512], P(('ty', 'tx')), may hold values from 1 to 128
- out_weight: bfloat16 [8192, 8192], P('tx', 'ty'), may hold values from -0.0625 to 0.0625
- final_gain: bfloat16 [8192], P(('ty', 'tx')), may hold values from 0.5 to 1.5
- in_weight: bfloat16 [8192, 2048], P('ty', 'tx'), may hold values from -0.0625 to 0.0625
- owners: int32 [512], replicated, may hold values from 0 to 31, as said below
- codebook_ids: int32 [512, 8], replicated, may hold values from 0 to 1023
- mlp_gate: bfloat16 [2048, 4096], P(None, 'tx'), may hold values from -0.125 to 0.125
- mlp_up: bfloat16 [2048, 4096], P(None, 'tx'), may hold values from -0.125 to 0.125
- mlp_down: bfloat16 [4096, 2048], P('tx'), may hold values from -0.09375 to 0.09375
- pre_gain: bfloat16 [2048], replicated, may hold values from 0.5 to 1.5
- head_gain: bfloat16 [2048], replicated, may hold values from 0.5 to 1.5
- codebook_table: bfloat16 [8, 1024, 2048], P(None, 'tx'), may hold values from -0.375 to 0.375
Outputs:
- hidden_out: bfloat16 [512, 8192], P(None, ('ty', 'tx'))
- depth_logprob: float32 [32, 8, 64], P('ty')
The draws below stay inside these ranges and needn't reach their ends.
Inputs may be any that keep to these rules, and one draw needn't show every extreme that they name: `owners`: in each of the 32 aligned blocks of 16 rows no owner is named more than 2 times, and one owner is named exactly 2 times in every block.
All inputs are finite; a program needn't handle non-finite values.
Results may differ from the reference program's by a relative error of at most 0.0095.
Values may be sent and summed in bfloat16 or wider, within the bound.
No kernel may reach another device: no remote copies, remote signals or barrier semaphores. Data moves between devices by JAX's collectives and lax.ppermute only.
A program may use at most 128 MiB of HBM per device.

```python
from functools import partial
import jax
import jax.numpy as jnp
from jax import lax

D = 8192
HEADS = 64
KV_HEADS = 8
HEAD_DIM = 128
DW = 2048
DFF = 4096
CB = 1024
STEPS = 8
LMAX = 128
QW = 8192
KW = 1024
QKVW = 10240
ROWS = 512
ROWS_TY = 16
OWNERS = 32
CAP = 2


def draw_hidden_in(key, part):
    key = jax.random.fold_in(key, 11)
    key_base, key_rows = jax.random.split(key, 2)
    row_scale = jnp.exp(jax.random.uniform(key_rows, (ROWS, 1), jnp.float32, jnp.log(0.3), jnp.log(3.0)))
    block_width = D // OWNERS
    column_pos = (jnp.arange(D, dtype=jnp.int32) % block_width).astype(jnp.float32) / (block_width - 1)
    base_values = jax.random.normal(key_base, (ROWS, D), jnp.float32)
    column_scale = 0.15 * jnp.exp(jnp.log(10.0) * column_pos)
    return (base_values * row_scale * column_scale[None, :]).astype(jnp.bfloat16)


def owner_block(hot_owner, block_key):
    key_order, key_pool = jax.random.split(block_key)
    other_pool = (hot_owner + 1 + jnp.arange((OWNERS - 1) * CAP, dtype=jnp.int32) // CAP) % OWNERS
    other_pool = jax.random.permutation(key_pool, other_pool)
    assigned = jnp.concatenate([jnp.full((CAP,), hot_owner, jnp.int32), other_pool[:ROWS_TY - CAP]])
    placing = jax.random.permutation(key_order, ROWS_TY)
    return assigned[jnp.argsort(placing)].astype(jnp.int32)


def draw_owners(key, part):
    key = jax.random.fold_in(key, 23)
    key_hot, key_blocks = jax.random.split(key)
    hot_owner = jax.random.randint(key_hot, (), 0, OWNERS, jnp.int32)
    block_keys = jax.random.split(key_blocks, OWNERS)
    return jax.vmap(partial(owner_block, hot_owner))(block_keys).reshape(ROWS)


def plant(drawn, rng, low, top_value):
    longest = drawn.shape.index(max(drawn.shape))
    spots = []
    for shift in (0, 1):
        where = [jax.random.randint(jax.random.fold_in(rng, axis), (), 0, length) for axis, length in enumerate(drawn.shape)]
        where[longest] = (where[longest] + shift) % drawn.shape[longest]
        spots.append(tuple(where))
    return drawn.at[spots[0]].set(low).at[spots[1]].set(top_value)


def level_of(rng, dims, pieces, least, largest):
    factor_of, own = 1.0, jax.random.fold_in(rng, 6)
    for axis_at, shards_of in pieces:
        draws = jnp.exp(jax.random.uniform(jax.random.fold_in(own, axis_at), (shards_of,), jnp.float32, least / len(pieces), largest / len(pieces)))
        factor_of = factor_of * jnp.repeat(draws, dims[axis_at] // shards_of).reshape([-1 if axis == axis_at else 1 for axis in range(len(dims))])
    return factor_of


def bell_draw(rng, extent, width, reach, shards=(), kind=jnp.bfloat16):
    array = width * jax.random.normal(rng, extent, jnp.float32)
    if shards:
        array = array * level_of(rng, extent, shards, -0.22, 0.18)
    return jnp.clip(array, -reach, reach).astype(kind)


def setup_inputs(seed: int = 0) -> dict:
    key_of = jax.random.split(jax.random.key(seed), 19)
    return {
        "hidden_in": draw_hidden_in(jax.random.fold_in(key_of[18], 71), 0),
        "norm_gain": jnp.clip(1.0 + 0.1 * jax.random.normal(key_of[1], (D,), jnp.float32), 0.5, 1.5).astype(jnp.bfloat16),
        "qkv_weight": bell_draw(key_of[2], (D, QKVW), D ** -0.5, 0.0625, ((0, 32), (1, 4))),
        "qkv_bias": bell_draw(key_of[3], (QKVW,), 1.0, 4.0),
        "key_cache": bell_draw(key_of[4], (ROWS, LMAX, KW), 1.0, 6.0, ((0, 128),)),
        "value_cache": bell_draw(key_of[5], (ROWS, LMAX, KW), 1.0, 6.0, ((0, 128),)),
        "lengths": plant(jax.random.randint(key_of[6], (ROWS,), 1, LMAX + 1), jax.random.fold_in(key_of[6], 1), 1, LMAX).astype(jnp.int32),
        "out_weight": bell_draw(key_of[7], (QW, D), QW ** -0.5, 0.0625, ((0, 4), (1, 32))),
        "final_gain": jnp.clip(1.0 + 0.1 * jax.random.normal(key_of[8], (D,), jnp.float32), 0.5, 1.5).astype(jnp.bfloat16),
        "in_weight": bell_draw(key_of[9], (D, DW), D ** -0.5, 0.0625, ((0, 32), (1, 4))),
        "owners": draw_owners(jax.random.fold_in(key_of[18], 71), 0),
        "codebook_ids": plant(jax.random.randint(key_of[11], (ROWS, STEPS), 0, CB), jax.random.fold_in(key_of[11], 1), 0, CB - 1).astype(jnp.int32),
        "mlp_gate": bell_draw(key_of[12], (DW, DFF), DW ** -0.5, 0.125, ((1, 4),)),
        "mlp_up": bell_draw(key_of[13], (DW, DFF), DW ** -0.5, 0.125, ((1, 4),)),
        "mlp_down": bell_draw(key_of[14], (DFF, DW), DFF ** -0.5, 0.09375, ((0, 4),)),
        "pre_gain": jnp.clip(1.0 + 0.1 * jax.random.normal(key_of[15], (DW,), jnp.float32), 0.5, 1.5).astype(jnp.bfloat16),
        "head_gain": jnp.clip(1.0 + 0.1 * jax.random.normal(key_of[16], (DW,), jnp.float32), 0.5, 1.5).astype(jnp.bfloat16),
        "codebook_table": bell_draw(key_of[17], (STEPS, CB, DW), (DW // 9) ** -0.5, 0.375, ((1, 4),)),
    }


epsilon = 1e-06
rope_base = 1000000.0
embed_gain = 16.0

def rms_scale(values, gain):
    mean_square = lax.optimization_barrier(jnp.mean(values * values, axis=-1, keepdims=True))
    return values * lax.rsqrt(mean_square + epsilon) * gain.astype(jnp.float32)

def rotate(values, position):
    half_dim = values.shape[-1] // 2
    frequency = jnp.exp(-jnp.log(rope_base) * (2.0 * jnp.arange(half_dim, dtype=jnp.float32) / values.shape[-1]))
    phase_angle = position.astype(jnp.float32)[:, None, None] * frequency[None, None, :]
    cosine = jnp.cos(phase_angle)
    sine_part = jnp.sin(phase_angle)
    first_half = values[..., :half_dim]
    second_half = values[..., half_dim:]
    return jnp.concatenate([first_half * cosine - second_half * sine_part, second_half * cosine + first_half * sine_part], axis=-1)

def attend(query_heads, new_key, new_value, key_cache, value_cache, lengths):
    row_count = query_heads.shape[0]
    group_size = HEADS // KV_HEADS
    query_heads = query_heads.reshape(row_count, KV_HEADS, group_size, HEAD_DIM).astype(jnp.float32)
    keys_all = key_cache.reshape(row_count, LMAX, KV_HEADS, HEAD_DIM).astype(jnp.float32)
    values_all = value_cache.reshape(row_count, LMAX, KV_HEADS, HEAD_DIM).astype(jnp.float32)
    scores = jnp.einsum('rgjd,rtgd->rgjt', query_heads, keys_all)
    own_score = jnp.einsum('rgjd,rgd->rgj', query_heads, new_key.astype(jnp.float32))
    in_cache = jnp.arange(LMAX, dtype=jnp.int32)[None, :] < lengths[:, None]
    weights = jnp.where(in_cache[:, None, None, :], jnp.exp(scores), 0.0)
    own_weight = jnp.exp(own_score)
    denominator = lax.optimization_barrier(jnp.sum(weights, axis=-1)) + own_weight
    probability = (weights / denominator[..., None]).astype(jnp.bfloat16)
    own_prob = (own_weight / denominator).astype(jnp.bfloat16)
    blended = jnp.einsum('rgjt,rtgd->rgjd', probability.astype(jnp.float32), values_all)
    blended = blended + own_prob.astype(jnp.float32)[..., None] * new_value.astype(jnp.float32)[:, :, None, :]
    return blended.reshape(row_count, HEADS * HEAD_DIM).astype(jnp.bfloat16)

def depth_rows(start_rows, codebook_ids, mlp_gate, mlp_up, mlp_down, pre_gain, head_gain, codebook_table):
    depth_state = start_rows.astype(jnp.float32)
    columns = []
    for step_index in range(STEPS):
        inner_rows = rms_scale(depth_state, pre_gain).astype(jnp.bfloat16)
        gate_part = jnp.dot(inner_rows, mlp_gate, preferred_element_type=jnp.float32)
        up_part = jnp.dot(inner_rows, mlp_up, preferred_element_type=jnp.float32)
        activation = (jax.nn.silu(gate_part) * up_part).astype(jnp.bfloat16)
        depth_state = depth_state + jnp.dot(activation, mlp_down, preferred_element_type=jnp.float32)
        outer_rows = rms_scale(depth_state, head_gain).astype(jnp.bfloat16)
        logits = jnp.dot(outer_rows, codebook_table[step_index].T, preferred_element_type=jnp.float32)
        picked = jnp.take_along_axis(logits, codebook_ids[:, step_index:step_index + 1], axis=1)[:, 0]
        columns.append(picked - jnp.log(lax.optimization_barrier(jnp.sum(jnp.exp(logits), axis=1))))
        if step_index + 1 < STEPS:
            embedded = codebook_table[step_index][codebook_ids[:, step_index]].astype(jnp.float32)
            depth_state = depth_state + embed_gain * embedded
    return jnp.stack(columns, axis=1)

def reference(hidden_in, norm_gain, qkv_weight, qkv_bias, key_cache, value_cache, lengths, out_weight, final_gain, in_weight, owners, codebook_ids, mlp_gate, mlp_up, mlp_down, pre_gain, head_gain, codebook_table):
    residual = hidden_in.astype(jnp.float32)
    normed = rms_scale(residual, norm_gain).astype(jnp.bfloat16)
    qkv_raw = jnp.dot(normed, qkv_weight, preferred_element_type=jnp.float32).astype(jnp.bfloat16)
    qkv = qkv_raw.astype(jnp.float32) + qkv_bias.astype(jnp.float32)
    query_width = HEADS * HEAD_DIM
    key_width = KV_HEADS * HEAD_DIM
    query_heads = rotate(qkv[:, :query_width].reshape(ROWS, HEADS, HEAD_DIM), lengths)
    query_heads = (query_heads * HEAD_DIM ** (-0.5)).astype(jnp.bfloat16)
    new_key = rotate(qkv[:, query_width:query_width + key_width].reshape(ROWS, KV_HEADS, HEAD_DIM), lengths).astype(jnp.bfloat16)
    new_value = qkv[:, query_width + key_width:].reshape(ROWS, KV_HEADS, HEAD_DIM).astype(jnp.bfloat16)
    attended = attend(query_heads, new_key, new_value, key_cache, value_cache, lengths)
    projected = jnp.dot(attended, out_weight, preferred_element_type=jnp.float32)
    hidden_out = (residual + projected).astype(jnp.bfloat16)
    final_rows = rms_scale(hidden_out.astype(jnp.float32), final_gain).astype(jnp.bfloat16)
    depth_start = jnp.dot(final_rows, in_weight, preferred_element_type=jnp.float32).astype(jnp.bfloat16)
    row_logprob = depth_rows(depth_start, codebook_ids, mlp_gate, mlp_up, mlp_down, pre_gain, head_gain, codebook_table)
    member = (owners[:, None] == jnp.arange(OWNERS, dtype=jnp.int32)[None, :]).astype(jnp.int32)
    earlier = jnp.cumsum(member.reshape(OWNERS, ROWS_TY, OWNERS), axis=1).reshape(ROWS, OWNERS) - member
    rank_in_block = lax.optimization_barrier(jnp.sum(earlier * member, axis=1))
    block_index = jnp.arange(ROWS, dtype=jnp.int32) // ROWS_TY
    slot_index = (block_index * CAP + rank_in_block).astype(jnp.int32)
    depth_logprob = jnp.zeros((OWNERS, STEPS, OWNERS * CAP), jnp.float32).at[owners, :, slot_index].set(row_logprob)
    return (hidden_out, depth_logprob)
```

```python
import jax
import jax.numpy as jnp
from jax import lax
from jax.experimental import pallas as pl
from jax.experimental.pallas import tpu as pltpu
from jax.sharding import PartitionSpec as P

HEADS = 64
KV_HEADS = 8
HEAD_DIM = 128
STEPS = 8
LMAX = 128
CAPACITY = 2
BF16 = jnp.bfloat16
F32 = jnp.float32


epsilon = 1e-06
rope_base = 1000000.0
embed_gain = 16.0


def rotate(values, position):
    half_dim = values.shape[-1] // 2
    frequency = jnp.exp(
        -jnp.log(rope_base) * (2.0 * jnp.arange(half_dim, dtype=F32) / values.shape[-1])
    )
    phase_angle = position.astype(F32)[:, None, None] * frequency[None, None, :]
    cosine = jnp.cos(phase_angle)
    sine_part = jnp.sin(phase_angle)
    first_half = values[..., :half_dim]
    second_half = values[..., half_dim:]
    return jnp.concatenate(
        [
            first_half * cosine - second_half * sine_part,
            second_half * cosine + first_half * sine_part,
        ],
        axis=-1,
    )


def attend(query_heads, new_key, new_value, key_cache, value_cache, lengths):
    row_count = query_heads.shape[0]
    group_size = HEADS // KV_HEADS
    query_heads = query_heads.reshape(row_count, KV_HEADS, group_size, HEAD_DIM)
    keys_all = key_cache.reshape(row_count, LMAX, KV_HEADS, HEAD_DIM)
    values_all = value_cache.reshape(row_count, LMAX, KV_HEADS, HEAD_DIM)
    scores = jnp.einsum("rgjd,rtgd->rgjt", query_heads, keys_all, preferred_element_type=F32)
    own_score = jnp.einsum("rgjd,rgd->rgj", query_heads, new_key, preferred_element_type=F32)
    in_cache = jnp.arange(LMAX, dtype=jnp.int32)[None, :] < lengths[:, None]
    weights = jnp.where(in_cache[:, None, None, :], jnp.exp(scores), 0.0)
    own_weight = jnp.exp(own_score)
    denominator = jnp.sum(weights, axis=-1) + own_weight
    probability = (weights / denominator[..., None]).astype(BF16)
    own_prob = (own_weight / denominator).astype(BF16)
    blended = jnp.einsum("rgjt,rtgd->rgjd", probability, values_all, preferred_element_type=F32)
    blended = blended + own_prob.astype(F32)[..., None] * new_value.astype(F32)[:, :, None, :]
    return blended.reshape(row_count, HEADS * HEAD_DIM).astype(BF16)


def flip(value, mask):
    return lax.ppermute(value, "tx", [(i, i ^ mask) for i in range(4)])


def swap(value):
    return lax.ppermute(value, "ty", [(i, i ^ 1) for i in range(32)])


def split_sum(values):
    high = values.astype(BF16)
    low = (values - high.astype(F32)).astype(BF16)
    return jnp.pad(jnp.stack([high, low], axis=-1), ((0, 0), (0, 126)))


def norm_rows(state, gain):
    mean_square = jnp.mean(state * state, axis=-1, keepdims=True)
    return (state * lax.rsqrt(mean_square + epsilon) * gain).astype(BF16)


def mlp(state, pre_gain, gate, up, down):
    inner = norm_rows(state, pre_gain[...].astype(F32))
    gate_part = jnp.dot(inner, gate[...], preferred_element_type=F32)
    up_part = jnp.dot(inner, up[...], preferred_element_type=F32)
    act = (gate_part / (1.0 + jnp.exp(-gate_part)) * up_part).astype(BF16)
    return jnp.dot(act, down[...], preferred_element_type=F32).astype(BF16)


def first_kernel(state, pre_gain, gate, up, down, part):
    part[...] = mlp(state[...], pre_gain, gate, up, down)


def total_of(state, parts):
    one, two, three, four = [part[...].astype(F32) for part in parts]
    return state[...] + ((one + two) + (three + four))


def middle_kernel(
    state, a, b, c, d, embed, pre_gain, head_gain, gate, up, down, outer, after, part
):
    total = total_of(state, (a, b, c, d))
    outer[...] = norm_rows(total, head_gain[...].astype(F32))
    total = total + embed_gain * embed[...].astype(F32)
    after[...] = total
    part[...] = mlp(total, pre_gain, gate, up, down)


def last_kernel(state, a, b, c, d, head_gain, outer):
    outer[...] = norm_rows(total_of(state, (a, b, c, d)), head_gain[...].astype(F32))


VMEM = pl.BlockSpec(memory_space=pltpu.VMEM)


def call(kernel, outs, weights, *operands, name):
    weights = [pltpu.with_memory_space_constraint(w, pltpu.VMEM) for w in weights]
    operands = operands + tuple(weights)
    size = sum(w.size for w in weights)
    return pl.pallas_call(
        kernel,
        out_shape=[jax.ShapeDtypeStruct(shape, dtype) for shape, dtype in outs],
        in_specs=[VMEM] * len(operands),
        out_specs=[VMEM] * len(outs),
        name=name,
        compiler_params=pltpu.CompilerParams(vmem_limit_bytes=16 * 2**20),
        cost_estimate=pl.CostEstimate(
            flops=32 * size, transcendentals=2**14, bytes_accessed=2 * size + 2**18
        ),
    )(*operands)


def body(
    hidden_in,
    norm_gain,
    qkv_weight,
    qkv_bias,
    key_cache,
    value_cache,
    lengths,
    out_weight,
    final_gain,
    in_weight,
    owners,
    codebook_ids,
    mlp_gate,
    mlp_up,
    mlp_down,
    pre_gain,
    head_gain,
    codebook_table,
):
    tx = lax.axis_index("tx")
    ty = lax.axis_index("ty")
    core = ty % 2
    rows, width = hidden_in.shape
    full_width = width * 128
    half = rows // 2
    devices = 128

    both = hidden_in.reshape(devices, 2, 2, width)
    kept = jnp.where(core == 0, both[:, 0], both[:, 1]).reshape(half, width)
    given = jnp.where(core == 0, both[:, 1], both[:, 0]).reshape(half, width)
    gains = jnp.pad(jnp.stack([norm_gain, final_gain]), ((0, 14), (0, 0)))
    taken = swap(jnp.concatenate([given, gains]))
    residual = jnp.concatenate([kept, taken[:half]], axis=1).astype(F32)
    gain_in = jnp.concatenate([norm_gain, taken[half]]).astype(F32)
    gain_out = jnp.concatenate([final_gain, taken[half + 1]]).astype(F32)
    scaled = (residual * gain_in).astype(BF16)
    squares = split_sum(jnp.sum(residual * residual, axis=1))

    def relative(value):
        return [
            lax.dynamic_index_in_dim(value, tx ^ mask, 0, keepdims=False) for mask in range(4)
        ]

    qkv_pair = jnp.stack([qkv_weight, swap(qkv_weight)])
    qkv_blocks = qkv_pair.reshape(2, 4, width, -1).transpose(1, 0, 2, 3)
    qkv_here = jnp.concatenate(relative(qkv_blocks)).reshape(8 * width, -1)
    gathered = jnp.concatenate(
        [scaled, flip(scaled, 1), flip(scaled, 2), flip(scaled, 3)], axis=1
    )
    partial_qkv = jnp.dot(gathered, qkv_here, preferred_element_type=F32).astype(BF16)
    sent = jnp.concatenate([partial_qkv, squares], axis=1).reshape(devices, 2, -1)
    got = lax.all_to_all(sent, ("ty", "tx"), 0, 0, tiled=True)
    got = jnp.sum(got.reshape(16, 2, 4, 2, -1).astype(F32), axis=0)
    columns = partial_qkv.shape[1]
    square_sum = jnp.sum(got[..., columns] + got[..., columns + 1], axis=1).reshape(4)
    scale = lax.rsqrt(square_sum / full_width + epsilon)
    qkv_raw = got[..., :columns].transpose(0, 2, 1, 3).reshape(4, 4 * columns)
    qkv_raw = (qkv_raw * scale[:, None]).astype(BF16)
    qkv = qkv_raw.astype(F32) + qkv_bias.astype(F32)
    query_width = HEADS * HEAD_DIM
    key_width = KV_HEADS * HEAD_DIM
    query_heads = rotate(qkv[:, :query_width].reshape(4, HEADS, HEAD_DIM), lengths)
    query_heads = (query_heads * HEAD_DIM ** (-0.5)).astype(BF16)
    new_key = rotate(
        qkv[:, query_width : query_width + key_width].reshape(4, KV_HEADS, HEAD_DIM), lengths
    ).astype(BF16)
    new_value = qkv[:, query_width + key_width :].reshape(4, KV_HEADS, HEAD_DIM).astype(BF16)
    attended = attend(query_heads, new_key, new_value, key_cache, value_cache, lengths)

    spread = attended.reshape(2, 2, 4, -1).transpose(0, 2, 1, 3)
    spread = jnp.broadcast_to(spread[None], (16,) + spread.shape).reshape(devices, 2, -1)
    spread = lax.all_to_all(spread, ("ty", "tx"), 0, 0, tiled=True).reshape(half, -1)
    out_pair = jnp.stack([out_weight, swap(out_weight)], axis=1)
    out_pair = out_pair.reshape(-1, 2, 4, width).transpose(2, 0, 1, 3)
    out_blocks = relative(out_pair.reshape(4, -1, 2 * width))
    pieces = [
        jnp.dot(spread, block, preferred_element_type=F32).astype(BF16) for block in out_blocks
    ]
    pieces = [pieces[0]] + [flip(pieces[mask], mask) for mask in (1, 2, 3)]
    pieces = [piece.astype(F32) for piece in pieces]
    projected = (pieces[0] + pieces[1]) + (pieces[2] + pieces[3])
    leaving = (residual + projected).astype(BF16)
    other = swap(leaving[:, width:]).reshape(devices, 1, 2, width)
    mine = leaving[:, :width].reshape(devices, 1, 2, width)
    hidden_out = jnp.where(
        core == 0,
        jnp.concatenate([mine, other], axis=1),
        jnp.concatenate([other, mine], axis=1),
    ).reshape(rows, width)

    in_blocks = relative(in_weight.reshape(4, width, -1))
    in_blocks = jnp.stack(
        [in_blocks[0]] + [flip(in_blocks[mask], mask) for mask in (1, 2, 3)]
    )
    in_own = jnp.concatenate(
        [lax.dynamic_index_in_dim(in_blocks, tx ^ place, 0, keepdims=False) for place in range(4)],
        axis=1,
    )
    in_here = jnp.concatenate([in_own, swap(in_own)])
    leaving = leaving.astype(F32)
    final_rows = (leaving * gain_out).astype(BF16)
    final_squares = split_sum(jnp.sum(leaving * leaving, axis=1))
    partial_start = jnp.dot(final_rows, in_here, preferred_element_type=F32).astype(BF16)
    sent = jnp.concatenate([partial_start, final_squares], axis=1).reshape(32, 8, -1)
    got = lax.all_to_all(sent, "ty", 0, 0, tiled=True)
    got = jnp.sum(got.reshape(16, 2, 4, 2, -1).astype(F32), axis=0)
    got = got.transpose(1, 0, 2, 3).reshape(16, -1)
    depth_width = partial_start.shape[1]
    square_part = split_sum(got[:, depth_width] + got[:, depth_width + 1])
    got = jnp.concatenate([got[:, :depth_width].astype(BF16), square_part], axis=1)
    parts = [part.astype(F32) for part in [got] + [flip(got, mask) for mask in (1, 2, 3)]]
    got = (parts[0] + parts[1]) + (parts[2] + parts[3])
    square_sum = got[:, depth_width : depth_width + 1] + got[:, depth_width + 1 : depth_width + 2]
    state = got[:, :depth_width] * lax.rsqrt(square_sum / full_width + epsilon)
    state = state.astype(BF16).astype(F32)

    block_rows = state.shape[0]
    entries = codebook_table.shape[1]
    codes = lax.dynamic_slice_in_dim(codebook_ids, ty * block_rows, block_rows, 0) - tx * entries
    chosen = codes.T[:, :, None] == jnp.arange(entries, dtype=jnp.int32)
    embeds = lax.dot_general(
        chosen[: STEPS - 1].astype(BF16),
        codebook_table[: STEPS - 1],
        (((2,), (1,)), ((0,), (0,))),
        preferred_element_type=F32,
    ).astype(BF16)
    embeds = embeds + flip(embeds, 1)
    embeds = embeds + flip(embeds, 3)
    pre_gain = pre_gain.reshape(1, -1)
    head_gain = head_gain.reshape(1, -1)
    weights = (mlp_gate, mlp_up, mlp_down)
    shape = state.shape
    (part,) = call(first_kernel, [(shape, BF16)], weights, state, pre_gain, name="depth_first")
    totals = []
    picks = []
    for step in range(STEPS):
        parts = [part] + [flip(part, mask) for mask in (1, 2, 3)]
        if step + 1 < STEPS:
            outer, state, part = call(
                middle_kernel,
                [(shape, BF16), (shape, F32), (shape, BF16)],
                weights,
                state,
                *parts,
                embeds[step],
                pre_gain,
                head_gain,
                name="depth_step",
            )
        else:
            (outer,) = call(
                last_kernel, [(shape, BF16)], (), state, *parts, head_gain, name="depth_last"
            )
        logits = lax.dot_general(
            outer, codebook_table[step], (((1,), (1,)), ((), ())), preferred_element_type=F32
        )
        totals.append(jnp.sum(jnp.exp(logits), axis=1))
        picks.append(jnp.sum(jnp.where(chosen[step], logits, 0.0), axis=1))
    found = jnp.stack(totals + picks, axis=1)

    owner_count = lax.axis_size("ty")
    block_owners = lax.dynamic_slice_in_dim(owners, ty * block_rows, block_rows, 0)
    same = block_owners[:, None] == block_owners[None, :]
    place = jnp.arange(block_rows)
    rank = jnp.sum((same & (place[None, :] < place[:, None])).astype(jnp.int32), axis=1)
    slot = block_owners * CAPACITY + rank
    select = slot[None, :] == jnp.arange(owner_count * CAPACITY, dtype=jnp.int32)[:, None]
    outgoing = jnp.sum(jnp.where(select[:, :, None], found[None], 0.0), axis=1)
    outgoing = outgoing.reshape(owner_count, 1, -1)
    outgoing = jnp.broadcast_to(outgoing, (owner_count, 4, outgoing.shape[2]))
    incoming = lax.all_to_all(
        outgoing.reshape(devices, -1), ("ty", "tx"), 0, 0, tiled=True
    )
    incoming = jnp.sum(incoming.reshape(owner_count, 4, -1), axis=1)
    incoming = incoming.reshape(owner_count * CAPACITY, 2, STEPS)
    filled = jnp.sum((owners == ty).reshape(owner_count, block_rows).astype(jnp.int32), axis=1)
    filled = (filled[:, None] > jnp.arange(CAPACITY)).reshape(-1, 1)
    logprob = jnp.where(filled, incoming[:, 1] - jnp.log(incoming[:, 0]), 0.0)
    return (hidden_out, logprob.T[None])


def solution(mesh):
    placed = (
        P(None, ("ty", "tx")),
        P(("ty", "tx")),
        P("ty", "tx"),
        P(),
        P(("ty", "tx"), None, None),
        P(("ty", "tx"), None, None),
        P(("ty", "tx")),
        P("tx", "ty"),
        P(("ty", "tx")),
        P("ty", "tx"),
        P(),
        P(),
        P(None, "tx"),
        P(None, "tx"),
        P("tx", None),
        P(),
        P(),
        P(None, "tx", None),
    )
    return jax.shard_map(
        body,
        mesh=mesh,
        in_specs=placed,
        out_specs=(P(None, ("ty", "tx")), P("ty", None, None)),
        check_vma=False,
    )
```

```python
import functools

import jax
import jax.numpy as jnp
from jax import lax
from jax.experimental import pallas as pl
from jax.experimental.pallas import tpu as pltpu
from jax.sharding import PartitionSpec as P

HEADS = 64
KV_HEADS = 8
HEAD_DIM = 128
STEPS = 8
LMAX = 128
CAPACITY = 2
ORDER = (2, 3, 1)
BF16 = jnp.bfloat16
F32 = jnp.float32


epsilon = 1e-06
rope_base = 1000000.0
embed_gain = 16.0


def rotate(values, position):
    half_dim = values.shape[-1] // 2
    frequency = jnp.exp(
        -jnp.log(rope_base) * (2.0 * jnp.arange(half_dim, dtype=F32) / values.shape[-1])
    )
    phase_angle = position.astype(F32)[:, None, None] * frequency[None, None, :]
    cosine = jnp.cos(phase_angle)
    sine_part = jnp.sin(phase_angle)
    first_half = values[..., :half_dim]
    second_half = values[..., half_dim:]
    return jnp.concatenate(
        [
            first_half * cosine - second_half * sine_part,
            second_half * cosine + first_half * sine_part,
        ],
        axis=-1,
    )


def attend(query_heads, new_key, new_value, key_cache, value_cache, lengths):
    row_count = query_heads.shape[0]
    group_size = HEADS // KV_HEADS
    query_heads = query_heads.reshape(row_count, KV_HEADS, group_size, HEAD_DIM)
    keys_all = key_cache.reshape(row_count, LMAX, KV_HEADS, HEAD_DIM)
    values_all = value_cache.reshape(row_count, LMAX, KV_HEADS, HEAD_DIM)
    scores = jnp.einsum("rgjd,rtgd->rgjt", query_heads, keys_all, preferred_element_type=F32)
    own_score = jnp.einsum("rgjd,rgd->rgj", query_heads, new_key, preferred_element_type=F32)
    in_cache = jnp.arange(LMAX, dtype=jnp.int32)[None, :] < lengths[:, None]
    weights = jnp.where(in_cache[:, None, None, :], jnp.exp(scores), 0.0)
    own_weight = jnp.exp(own_score)
    denominator = jnp.sum(weights, axis=-1) + own_weight
    probability = (weights / denominator[..., None]).astype(BF16)
    own_prob = (own_weight / denominator).astype(BF16)
    blended = jnp.einsum("rgjt,rtgd->rgjd", probability, values_all, preferred_element_type=F32)
    blended = blended + own_prob.astype(F32)[..., None] * new_value.astype(F32)[:, :, None, :]
    return blended.reshape(row_count, HEADS * HEAD_DIM).astype(BF16)


def flip(value, mask):
    return lax.ppermute(value, "tx", [(i, i ^ mask) for i in range(4)])


def with_others(value):
    return [value] + [flip(value, mask) for mask in ORDER]


def swap(value):
    return lax.ppermute(value, "ty", [(i, i ^ 1) for i in range(32)])


def split_sum(values):
    high = values.astype(BF16)
    low = (values - high.astype(F32)).astype(BF16)
    return jnp.pad(jnp.stack([high, low], axis=-1), ((0, 0), (0, 126)))


def norm_rows(state, gain):
    mean_square = jnp.mean(state * state, axis=-1, keepdims=True)
    return (state * lax.rsqrt(mean_square + epsilon) * gain).astype(BF16)


def hidden(state, pre_gain, gate, up):
    inner = norm_rows(state, pre_gain[...].astype(F32))
    gate_part = jnp.dot(inner, gate[...], preferred_element_type=F32)
    up_part = jnp.dot(inner, up[...], preferred_element_type=F32)
    return (gate_part / (1.0 + jnp.exp(-gate_part)) * up_part).astype(BF16)


def mlp(state, pre_gain, gate, up, down):
    act = hidden(state, pre_gain, gate, up)
    return jnp.dot(act, down[...], preferred_element_type=F32).astype(BF16)


def total_of(parts):
    one, two, three, four = [part[...].astype(F32) for part in parts]
    return (one + four) + (two + three)


def load_kernel(gate, up, after, gate_out, up_out, sems):
    copies = [
        pltpu.make_async_copy(gate, gate_out, sems.at[0]),
        pltpu.make_async_copy(up, up_out, sems.at[1]),
    ]
    for copy in copies:
        copy.start()
    for copy in copies:
        copy.wait()


def in_hbm(value):
    return pltpu.with_memory_space_constraint(value, pltpu.HBM)


def load(gate, up, after):
    return pl.pallas_call(
        load_kernel,
        out_shape=[pltpu.VMEM(gate.shape, BF16), pltpu.VMEM(up.shape, BF16)],
        in_specs=[HBM] * 3,
        out_specs=[VMEM] * 2,
        scratch_shapes=[pltpu.SemaphoreType.DMA((2,))],
        name="depth_weights",
        compiler_params=pltpu.CompilerParams(vmem_limit_bytes=2**20),
        cost_estimate=pl.CostEstimate(
            flops=0, transcendentals=0, bytes_accessed=4 * (gate.size + up.size)
        ),
    )(in_hbm(gate), in_hbm(up), in_hbm(after))


def fold_kernel(chips, out):
    count, rows, columns = chips.shape
    width = columns - 128
    halves = []
    for core in range(2):
        total = chips[core].astype(F32)
        for chip in range(1, count // 2):
            total = total + chips[2 * chip + core].astype(F32)
        halves.append(total)
    total = jnp.concatenate(halves, axis=0)
    out[:, :width] = total[:, :width].astype(BF16)
    square = total[:, width : width + 1] + total[:, width + 1 : width + 2]
    high = square.astype(BF16).astype(F32)
    lane = lax.broadcasted_iota(jnp.int32, (2 * rows, 128), 1)
    tail = jnp.where(lane == 0, high, jnp.where(lane == 1, square - high, 0.0))
    out[:, width:] = tail.astype(BF16)


def first_kernel(
    full_width, a, b, c, d, codes, slots, pre_gain, gate, up, down,
    state, part, codes_out, slots_out, found, down_out, sem,
):
    copy = pltpu.make_async_copy(down, down_out, sem)
    copy.start()
    total = total_of((a, b, c, d))
    width = state.shape[1]
    square = total[:, width : width + 1] + total[:, width + 1 : width + 2]
    start = total[:, :width] * lax.rsqrt(square / full_width + epsilon)
    start = start.astype(BF16).astype(F32)
    state[...] = start
    codes_out[...] = codes[...]
    slots_out[...] = slots[...]
    found[...] = jnp.zeros(found.shape, F32)
    act = hidden(start, pre_gain, gate, up)
    copy.wait()
    part[...] = jnp.dot(act, down_out[...], preferred_element_type=F32).astype(BF16)


def score(step, outer, codes, table, found):
    logits = lax.dot_general(
        outer, table, (((1,), (1,)), ((), ())), preferred_element_type=F32
    )
    entry = lax.broadcasted_iota(jnp.int32, logits.shape, 1)
    chosen = codes[:, step : step + 1] == entry
    picked = jnp.sum(jnp.where(chosen, logits, 0.0), axis=1, keepdims=True)
    exp_total = jnp.sum(jnp.exp(logits), axis=1, keepdims=True)
    lane = lax.broadcasted_iota(jnp.int32, found.shape, 1)
    kept = jnp.where(lane == step, exp_total, found[...])
    return jnp.where(lane == STEPS + step, picked, kept)


def score_kernel(step, outer, codes, found, table, out, entries, sem):
    copy = pltpu.make_async_copy(table.at[step], entries, sem.at[0])
    copy.start()
    copy.wait()
    out[...] = score(step, outer[...], codes, entries[...], found)


def score_first_kernel(step, outer, codes, found, table, out, last, entries, sem):
    copy = pltpu.make_async_copy(table.at[STEPS - 1], last, sem.at[1])
    copy.start()
    score_kernel(step, outer, codes, found, table, out, entries, sem)
    copy.wait()


def middle_kernel(
    step, state, a, b, c, d, found, left, right, pre_gain, head_gain, gate, up, down,
    after, part, outer,
):
    total = state[...] + total_of((a, b, c, d))
    outer[...] = norm_rows(total, head_gain[...].astype(F32))
    embed = jnp.concatenate([left[step], right[step]], axis=1)
    total = total + embed_gain * embed.astype(F32)
    after[...] = total
    part[...] = mlp(total, pre_gain, gate, up, down)


def last_kernel(step, state, a, b, c, d, found, codes, slots, head_gain, table, other, out, kept):
    total = state[...] + total_of((a, b, c, d))
    outer = norm_rows(total, head_gain[...].astype(F32))
    done = score(step, outer, codes, table[...], found)
    lane = lax.broadcasted_iota(jnp.int32, done.shape, 1)
    done = jnp.where(lane == 2 * STEPS, 1.0, done)
    done = done + pltpu.roll(done, 128 // 4, 1)
    owner_count = out.shape[0]
    shape = (owner_count, 128)
    lane = lax.broadcasted_iota(jnp.int32, shape, 1)
    target = CAPACITY * lax.broadcasted_iota(jnp.int32, shape, 0) + lane // (128 // 4)
    result = jnp.zeros(shape, F32)
    for row in range(state.shape[0]):
        result = result + jnp.where(target == slots[row : row + 1, :], done[row : row + 1], 0.0)
    out[...] = jnp.broadcast_to(result[:, None, :], out.shape)
    kept[...] = other[...]


VMEM = pl.BlockSpec(memory_space=pltpu.VMEM)
HBM = pl.BlockSpec(memory_space=pltpu.HBM)


def call(kernel, outs, *operands, name, specs=None, grid=(), scratch=()):
    size = sum(w.size for w in operands)
    return pl.pallas_call(
        kernel,
        out_shape=[jax.ShapeDtypeStruct(*out) if type(out) is tuple else out for out in outs],
        grid=grid,
        in_specs=specs or [VMEM] * len(operands),
        out_specs=[VMEM] * len(outs),
        scratch_shapes=scratch,
        name=name,
        compiler_params=pltpu.CompilerParams(vmem_limit_bytes=8 * 2**20),
        cost_estimate=pl.CostEstimate(
            flops=32 * size, transcendentals=2**14, bytes_accessed=2 * size + 2**18
        ),
    )(*operands)


def body(
    hidden_in,
    norm_gain,
    qkv_weight,
    qkv_bias,
    key_cache,
    value_cache,
    lengths,
    out_weight,
    final_gain,
    in_weight,
    owners,
    codebook_ids,
    mlp_gate,
    mlp_up,
    mlp_down,
    pre_gain,
    head_gain,
    codebook_table,
):
    tx = lax.axis_index("tx")
    ty = lax.axis_index("ty")
    core = ty % 2
    rows, width = hidden_in.shape
    full_width = width * 128
    half = rows // 2
    devices = 128

    both = hidden_in.reshape(devices, 2, 2, width)
    kept = jnp.where(core == 0, both[:, 0], both[:, 1]).reshape(half, width)
    given = jnp.where(core == 0, both[:, 1], both[:, 0]).reshape(half, width)
    gains = jnp.pad(jnp.stack([norm_gain, final_gain]), ((0, 14), (0, 0)))
    taken = swap(jnp.concatenate([given, gains]))
    residual = jnp.concatenate([kept, taken[:half]], axis=1).astype(F32)
    gain_in = jnp.concatenate([norm_gain, taken[half]]).astype(F32)
    gain_out = jnp.concatenate([final_gain, taken[half + 1]]).astype(F32)
    scaled = (residual * gain_in).astype(BF16)
    squares = split_sum(jnp.sum(residual * residual, axis=1))

    def relative(value):
        return [
            lax.dynamic_index_in_dim(value, tx ^ mask, 0, keepdims=False) for mask in (0,) + ORDER
        ]

    qkv_pair = jnp.stack([qkv_weight, swap(qkv_weight)])
    qkv_blocks = qkv_pair.reshape(2, 4, width, -1).transpose(1, 0, 2, 3)
    qkv_here = jnp.concatenate(relative(qkv_blocks)).reshape(8 * width, -1)
    gathered = jnp.concatenate(with_others(scaled), axis=1)
    partial_qkv = jnp.dot(gathered, qkv_here, preferred_element_type=F32).astype(BF16)
    sent = jnp.concatenate([partial_qkv, squares], axis=1).reshape(devices, 2, -1)
    got = lax.all_to_all(sent, ("ty", "tx"), 0, 0, tiled=True)
    got = jnp.sum(got.reshape(16, 2, 4, 2, -1).astype(F32), axis=0)
    columns = partial_qkv.shape[1]
    square_sum = jnp.sum(got[..., columns] + got[..., columns + 1], axis=1).reshape(4)
    scale = lax.rsqrt(square_sum / full_width + epsilon)
    qkv_raw = got[..., :columns].transpose(0, 2, 1, 3).reshape(4, 4 * columns)
    qkv_raw = (qkv_raw * scale[:, None]).astype(BF16)
    qkv = qkv_raw.astype(F32) + qkv_bias.astype(F32)
    query_width = HEADS * HEAD_DIM
    key_width = KV_HEADS * HEAD_DIM
    query_heads = rotate(qkv[:, :query_width].reshape(4, HEADS, HEAD_DIM), lengths)
    query_heads = (query_heads * HEAD_DIM ** (-0.5)).astype(BF16)
    new_key = rotate(
        qkv[:, query_width : query_width + key_width].reshape(4, KV_HEADS, HEAD_DIM), lengths
    ).astype(BF16)
    new_value = qkv[:, query_width + key_width :].reshape(4, KV_HEADS, HEAD_DIM).astype(BF16)
    attended = attend(query_heads, new_key, new_value, key_cache, value_cache, lengths)

    spread = attended.reshape(2, 2, 4, -1).transpose(0, 2, 1, 3)
    spread = jnp.broadcast_to(spread[None], (16,) + spread.shape).reshape(devices, 2, -1)
    spread = lax.all_to_all(spread, ("ty", "tx"), 0, 0, tiled=True).reshape(half, -1)
    out_pair = jnp.stack([out_weight, swap(out_weight)], axis=1)
    out_pair = out_pair.reshape(-1, 2, 4, width).transpose(2, 0, 1, 3)
    out_here = jnp.concatenate(relative(out_pair.reshape(4, -1, 2 * width)), axis=1)
    partial_out = jnp.dot(spread, out_here, preferred_element_type=F32).astype(BF16)
    pieces = jnp.split(partial_out, 4, axis=1)
    pieces = [pieces[0]] + [flip(piece, mask) for piece, mask in zip(pieces[1:], ORDER)]
    pieces = [piece.astype(F32) for piece in pieces]
    projected = (pieces[0] + pieces[3]) + (pieces[1] + pieces[2])
    leaving = (residual + projected).astype(BF16)
    other = swap(leaving[:, width:])

    in_blocks = relative(in_weight.reshape(4, width, -1))
    in_blocks = [in_blocks[0]] + [flip(b, mask) for b, mask in zip(in_blocks[1:], ORDER)]
    in_blocks = jnp.stack([in_blocks[((0,) + ORDER).index(mask)] for mask in range(4)])
    in_own = jnp.concatenate(
        [lax.dynamic_index_in_dim(in_blocks, tx ^ place, 0, keepdims=False) for place in range(4)],
        axis=1,
    )
    in_here = jnp.concatenate([in_own, swap(in_own)])
    exact = leaving.astype(F32)
    final_rows = (exact * gain_out).astype(BF16)
    final_squares = split_sum(jnp.sum(exact * exact, axis=1))
    partial_start = jnp.dot(final_rows, in_here, preferred_element_type=F32).astype(BF16)
    sent = jnp.concatenate([partial_start, final_squares], axis=1).reshape(32, 8, -1)
    got = lax.all_to_all(sent, "ty", 0, 0, tiled=True)
    (got,) = call(fold_kernel, [((16, sent.shape[2]), BF16)], got, name="fold")
    starts = with_others(got)
    depth_width = partial_start.shape[1]

    block_rows = got.shape[0]
    entries = codebook_table.shape[1]

    def by_core(value):
        return value.reshape(4, 2, 2, -1).transpose(1, 0, 2, 3).reshape(block_rows, -1)

    codes = lax.dynamic_slice_in_dim(codebook_ids, ty * block_rows, block_rows, 0)
    codes = by_core(codes) - tx * entries
    chosen = codes.T[: STEPS - 1, :, None] == jnp.arange(entries, dtype=jnp.int32)
    embeds = lax.dot_general(
        chosen.astype(BF16),
        codebook_table[: STEPS - 1],
        (((2,), (1,)), ((0,), (0,))),
        preferred_element_type=F32,
    ).astype(BF16)
    sides = jnp.split(embeds, 2, axis=2)
    sides = [side + flip(side, mask) for side, mask in zip(sides, (1, 3))]
    sides = [side + flip(side, mask) for side, mask in zip(sides, (3, 1))]
    owner_count = lax.axis_size("ty")
    block_owners = lax.dynamic_slice_in_dim(owners, ty * block_rows, block_rows, 0)
    same = block_owners[:, None] == block_owners[None, :]
    place = jnp.arange(block_rows)
    rank = jnp.sum((same & (place[None, :] < place[:, None])).astype(jnp.int32), axis=1)
    slots = by_core(block_owners * CAPACITY + rank)
    pre_gain = pre_gain.reshape(1, -1)
    head_gain = head_gain.reshape(1, -1)
    gate, up = load(mlp_gate, mlp_up, got)
    shape = (block_rows, depth_width)
    state, part, codes, slots, found, down = call(
        functools.partial(first_kernel, full_width),
        [
            (shape, F32),
            (shape, BF16),
            (codes.shape, jnp.int32),
            (slots.shape, jnp.int32),
            ((block_rows, 128), F32),
            pltpu.VMEM(mlp_down.shape, BF16),
        ],
        *starts,
        codes,
        slots,
        pre_gain,
        gate,
        up,
        in_hbm(mlp_down),
        name="depth_first",
        specs=[VMEM] * 9 + [HBM],
        scratch=[pltpu.SemaphoreType.DMA],
    )
    table_shape = codebook_table.shape[1:]
    for step in range(STEPS - 1):
        parts = with_others(part)
        state, part, outer = call(
            functools.partial(middle_kernel, step),
            [(shape, F32), (shape, BF16), (shape, BF16)],
            state,
            *parts,
            found,
            *sides,
            pre_gain,
            head_gain,
            gate,
            up,
            down,
            name="depth_step",
        )
        found, *extra = call(
            functools.partial(score_kernel if step else score_first_kernel, step),
            [(found.shape, F32)] + [pltpu.VMEM(table_shape, BF16)] * (step == 0),
            outer,
            codes,
            found,
            in_hbm(codebook_table),
            name="depth_score",
            specs=[VMEM] * 3 + [HBM],
            scratch=[pltpu.VMEM(table_shape, BF16), pltpu.SemaphoreType.DMA((2,))],
        )
        if step == 0:
            (last_table,) = extra
    parts = with_others(part)
    outgoing, other = call(
        functools.partial(last_kernel, STEPS - 1),
        [((owner_count, 4, 128), F32), (other.shape, BF16)],
        state,
        *parts,
        found,
        codes,
        slots,
        head_gain,
        last_table,
        other,
        name="depth_last",
    )

    incoming = lax.all_to_all(outgoing.reshape(devices, 128), ("ty", "tx"), 0, 0, tiled=True)
    other = other.reshape(devices, 1, 2, width)
    mine = leaving[:, :width].reshape(devices, 1, 2, width)
    hidden_out = jnp.where(
        core == 0,
        jnp.concatenate([mine, other], axis=1),
        jnp.concatenate([other, mine], axis=1),
    ).reshape(rows, width)
    incoming = jnp.sum(incoming.reshape(owner_count, 4, -1), axis=1)
    incoming = incoming[:, : 128 // 2].reshape(owner_count * CAPACITY, -1)
    logprob = incoming[:, STEPS : 2 * STEPS] - jnp.log(incoming[:, :STEPS])
    logprob = jnp.where(incoming[:, 2 * STEPS : 2 * STEPS + 1] > 0.0, logprob, 0.0)
    return (hidden_out, logprob.T[None])


def solution(mesh):
    placed = (
        P(None, ("ty", "tx")),
        P(("ty", "tx")),
        P("ty", "tx"),
        P(),
        P(("ty", "tx"), None, None),
        P(("ty", "tx"), None, None),
        P(("ty", "tx")),
        P("tx", "ty"),
        P(("ty", "tx")),
        P("ty", "tx"),
        P(),
        P(),
        P(None, "tx"),
        P(None, "tx"),
        P("tx", None),
        P(),
        P(),
        P(None, "tx", None),
    )
    return jax.shard_map(
        body,
        mesh=mesh,
        in_specs=placed,
        out_specs=(P(None, ("ty", "tx")), P("ty", None, None)),
        check_vma=False,
    )
```

```python
import functools

import jax
import jax.numpy as jnp
from jax import lax
from jax.experimental import pallas as pl
from jax.experimental.pallas import tpu as pltpu
from jax.sharding import PartitionSpec as P

HEADS = 64
KV_HEADS = 8
HEAD_DIM = 128
STEPS = 8
LMAX = 128
CAPACITY = 2
ORDER = (2, 3, 1)
BF16 = jnp.bfloat16
F32 = jnp.float32


epsilon = 1e-06
rope_base = 1000000.0
embed_gain = 16.0


def rotation(position):
    half_dim = HEAD_DIM // 2
    frequency = jnp.exp(
        -jnp.log(rope_base) * (2.0 * jnp.arange(half_dim, dtype=F32) / HEAD_DIM)
    )
    phase_angle = position.astype(F32)[:, None] * frequency[None, :]
    cosine = jnp.cos(phase_angle)
    sine = jnp.sin(phase_angle)
    return (
        jnp.concatenate([cosine, cosine], axis=1),
        jnp.concatenate([-sine, sine], axis=1),
    )


def attend_kernel(
    full_width, sums, bias, cosine, sine, lengths, keys, values,
    out, heads, scores, blocks, key_here, value_here, sems,
):
    copies = [
        pltpu.make_async_copy(keys, key_here, sems.at[0]),
        pltpu.make_async_copy(values, value_here, sems.at[1]),
    ]
    for copy in copies:
        copy.start()
    units = HEADS + 2 * KV_HEADS
    group = HEADS // KV_HEADS
    per_tx = units // 4
    width = per_tx * HEAD_DIM
    for core in range(2):
        block = sums[8 * core : 8 * core + 8, :]
        square = block[:, width : width + 1] + block[:, width + 1 : width + 2]
        first = jnp.sum(square[:4], axis=0, keepdims=True)
        second = jnp.sum(square[4:], axis=0, keepdims=True)
        place = lax.broadcasted_iota(jnp.int32, (8, 1), 0)
        scale = lax.rsqrt(jnp.where(place < 4, first, second) / full_width + epsilon)
        for unit in range(per_tx):
            piece = block[:, unit * HEAD_DIM : (unit + 1) * HEAD_DIM] * scale
            heads[pl.ds(2 * core * units + unit, 8, stride=per_tx), :] = piece
    queries = []
    owns = []
    news = []
    for row in range(4):
        raw = heads[row * units : (row + 1) * units, :].astype(BF16).astype(F32) + bias[...]
        turned = raw * cosine[row : row + 1, :] + pltpu.roll(raw, HEAD_DIM // 2, 1) * (
            sine[row : row + 1, :]
        )
        query = (turned[:HEADS] * HEAD_DIM ** (-0.5)).astype(BF16)
        new_key = turned[HEADS : HEADS + KV_HEADS].astype(BF16).astype(F32)
        new_value = raw[HEADS + KV_HEADS :].astype(BF16).astype(F32)
        spread_key = jnp.concatenate(
            [jnp.broadcast_to(new_key[h : h + 1], (group, HEAD_DIM)) for h in range(KV_HEADS)]
        )
        query = query.astype(F32)
        queries.append(query)
        owns.append(jnp.sum(query * spread_key, axis=1, keepdims=True))
        news.append(new_value)
    copies[0].wait()
    for row in range(4):
        for head in range(KV_HEADS):
            part = slice(head * group, (head + 1) * group)
            scores[row * HEADS + head * group : row * HEADS + (head + 1) * group, :] = (
                lax.dot_general(
                    queries[row][part].astype(BF16),
                    key_here[row, :, head * HEAD_DIM : (head + 1) * HEAD_DIM],
                    (((1,), (1,)), ((), ())),
                    preferred_element_type=F32,
                )
            )
    copies[1].wait()
    slot = lax.broadcasted_iota(jnp.int32, (HEADS, LMAX), 1)
    for row in range(4):
        rows = slice(row * HEADS, (row + 1) * HEADS)
        weights = jnp.where(slot < lengths[row : row + 1, :], jnp.exp(scores[rows, :]), 0.0)
        own_weight = jnp.exp(owns[row])
        denominator = jnp.sum(weights, axis=1, keepdims=True) + own_weight
        probability = (weights / denominator).astype(BF16).astype(F32)
        own_prob = (own_weight / denominator).astype(BF16).astype(F32)
        for head in range(KV_HEADS):
            part = slice(head * group, (head + 1) * group)
            blended = jnp.dot(
                probability[part].astype(BF16),
                value_here[row, :, head * HEAD_DIM : (head + 1) * HEAD_DIM],
                preferred_element_type=F32,
            )
            heads[row * HEADS + head * group : row * HEADS + (head + 1) * group, :] = (
                blended + own_prob[part] * news[row][head : head + 1]
            )
    for core in range(2):
        for head in range(HEADS):
            tx, place = divmod(head, HEADS // 4)
            both = heads[pl.ds(2 * core * HEADS + head, 2, stride=HEADS), :]
            blocks[4 * core + tx, :, place * HEAD_DIM : (place + 1) * HEAD_DIM] = both.astype(BF16)
    copies = [
        pltpu.make_async_copy(blocks, out.at[pl.ds(8 * chip, 8)], sems.at[chip])
        for chip in range(out.shape[0] // 8)
    ]
    for copy in copies:
        copy.start()
    for copy in copies:
        copy.wait()


def flip(value, mask):
    return lax.ppermute(value, "tx", [(i, i ^ mask) for i in range(4)])


def with_others(value):
    return [value] + [flip(value, mask) for mask in ORDER]


def swap(value):
    return lax.ppermute(value, "ty", [(i, i ^ 1) for i in range(32)])


def split_sum(values):
    high = values.astype(BF16)
    low = (values - high.astype(F32)).astype(BF16)
    return jnp.pad(jnp.stack([high, low], axis=-1), ((0, 0), (0, 126)))


def norm_rows(state, gain):
    mean_square = jnp.mean(state * state, axis=-1, keepdims=True)
    return (state * lax.rsqrt(mean_square + epsilon) * gain).astype(BF16)


def hidden(state, pre_gain, gate, up):
    inner = norm_rows(state, pre_gain[...].astype(F32))
    gate_part = jnp.dot(inner, gate[...], preferred_element_type=F32)
    up_part = jnp.dot(inner, up[...], preferred_element_type=F32)
    return (gate_part / (1.0 + jnp.exp(-gate_part)) * up_part).astype(BF16)


def mlp(state, pre_gain, gate, up, down):
    act = hidden(state, pre_gain, gate, up)
    return jnp.dot(act, down[...], preferred_element_type=F32).astype(BF16)


def total_of(parts):
    one, two, three, four = [part[...].astype(F32) for part in parts]
    return (one + four) + (two + three)


def load_kernel(gate, up, after, gate_out, up_out, sems):
    copies = [
        pltpu.make_async_copy(gate, gate_out, sems.at[0]),
        pltpu.make_async_copy(up, up_out, sems.at[1]),
    ]
    for copy in copies:
        copy.start()
    for copy in copies:
        copy.wait()


def in_hbm(value):
    return pltpu.with_memory_space_constraint(value, pltpu.HBM)


def load(gate, up, after):
    return pl.pallas_call(
        load_kernel,
        out_shape=[pltpu.VMEM(gate.shape, BF16), pltpu.VMEM(up.shape, BF16)],
        in_specs=[HBM] * 3,
        out_specs=[VMEM] * 2,
        scratch_shapes=[pltpu.SemaphoreType.DMA((2,))],
        name="depth_weights",
        compiler_params=pltpu.CompilerParams(vmem_limit_bytes=2**20),
        cost_estimate=pl.CostEstimate(
            flops=0, transcendentals=0, bytes_accessed=4 * (gate.size + up.size)
        ),
    )(in_hbm(gate), in_hbm(up), in_hbm(after))


def fold_kernel(chips, out):
    count, rows, columns = chips.shape
    width = columns - 128
    halves = []
    for core in range(2):
        total = chips[core].astype(F32)
        for chip in range(1, count // 2):
            total = total + chips[2 * chip + core].astype(F32)
        halves.append(total)
    total = jnp.concatenate(halves, axis=0)
    out[:, :width] = total[:, :width].astype(BF16)
    square = total[:, width : width + 1] + total[:, width + 1 : width + 2]
    high = square.astype(BF16).astype(F32)
    lane = lax.broadcasted_iota(jnp.int32, (2 * rows, 128), 1)
    tail = jnp.where(lane == 0, high, jnp.where(lane == 1, square - high, 0.0))
    out[:, width:] = tail.astype(BF16)


def first_kernel(
    full_width, a, b, c, d, codes, slots, pre_gain, gate, up, down,
    state, part, codes_out, slots_out, found, down_out, sem,
):
    copy = pltpu.make_async_copy(down, down_out, sem)
    copy.start()
    total = total_of((a, b, c, d))
    width = state.shape[1]
    square = total[:, width : width + 1] + total[:, width + 1 : width + 2]
    start = total[:, :width] * lax.rsqrt(square / full_width + epsilon)
    start = start.astype(BF16).astype(F32)
    state[...] = start
    codes_out[...] = codes[...]
    slots_out[...] = slots[...]
    found[...] = jnp.zeros(found.shape, F32)
    act = hidden(start, pre_gain, gate, up)
    copy.wait()
    part[...] = jnp.dot(act, down_out[...], preferred_element_type=F32).astype(BF16)


def score(step, outer, codes, table, found):
    logits = lax.dot_general(
        outer, table, (((1,), (1,)), ((), ())), preferred_element_type=F32
    )
    entry = lax.broadcasted_iota(jnp.int32, logits.shape, 1)
    chosen = codes[:, step : step + 1] == entry
    picked = jnp.sum(jnp.where(chosen, logits, 0.0), axis=1, keepdims=True)
    exp_total = jnp.sum(jnp.exp(logits), axis=1, keepdims=True)
    lane = lax.broadcasted_iota(jnp.int32, found.shape, 1)
    kept = jnp.where(lane == step, exp_total, found[...])
    return jnp.where(lane == STEPS + step, picked, kept)


def score_kernel(step, outer, codes, found, table, out, entries, sem):
    copy = pltpu.make_async_copy(table.at[step], entries, sem.at[0])
    copy.start()
    copy.wait()
    out[...] = score(step, outer[...], codes, entries[...], found)


def score_first_kernel(step, outer, codes, found, table, out, last, entries, sem):
    copy = pltpu.make_async_copy(table.at[STEPS - 1], last, sem.at[1])
    copy.start()
    score_kernel(step, outer, codes, found, table, out, entries, sem)
    copy.wait()


def middle_kernel(
    step, state, a, b, c, d, found, left, right, pre_gain, head_gain, gate, up, down,
    after, part, outer,
):
    total = state[...] + total_of((a, b, c, d))
    outer[...] = norm_rows(total, head_gain[...].astype(F32))
    embed = jnp.concatenate([left[step], right[step]], axis=1)
    total = total + embed_gain * embed.astype(F32)
    after[...] = total
    part[...] = mlp(total, pre_gain, gate, up, down)


def last_kernel(step, state, a, b, c, d, found, codes, slots, head_gain, table, other, out, kept):
    total = state[...] + total_of((a, b, c, d))
    outer = norm_rows(total, head_gain[...].astype(F32))
    done = score(step, outer, codes, table[...], found)
    lane = lax.broadcasted_iota(jnp.int32, done.shape, 1)
    done = jnp.where(lane == 2 * STEPS, 1.0, done)
    done = done + pltpu.roll(done, 128 // 4, 1)
    owner_count = out.shape[0]
    shape = (owner_count, 128)
    lane = lax.broadcasted_iota(jnp.int32, shape, 1)
    target = CAPACITY * lax.broadcasted_iota(jnp.int32, shape, 0) + lane // (128 // 4)
    result = jnp.zeros(shape, F32)
    for row in range(state.shape[0]):
        result = result + jnp.where(target == slots[row : row + 1, :], done[row : row + 1], 0.0)
    out[...] = jnp.broadcast_to(result[:, None, :], out.shape)
    kept[...] = other[...]


VMEM = pl.BlockSpec(memory_space=pltpu.VMEM)
HBM = pl.BlockSpec(memory_space=pltpu.HBM)


def call(kernel, outs, *operands, name, specs=None, out_specs=None, scratch=()):
    size = sum(w.size for w in operands)
    return pl.pallas_call(
        kernel,
        out_shape=[jax.ShapeDtypeStruct(*out) if type(out) is tuple else out for out in outs],
        in_specs=specs or [VMEM] * len(operands),
        out_specs=out_specs or [VMEM] * len(outs),
        scratch_shapes=scratch,
        name=name,
        compiler_params=pltpu.CompilerParams(vmem_limit_bytes=8 * 2**20),
        cost_estimate=pl.CostEstimate(
            flops=32 * size, transcendentals=2**14, bytes_accessed=2 * size + 2**18
        ),
    )(*operands)


def body(
    hidden_in,
    norm_gain,
    qkv_weight,
    qkv_bias,
    key_cache,
    value_cache,
    lengths,
    out_weight,
    final_gain,
    in_weight,
    owners,
    codebook_ids,
    mlp_gate,
    mlp_up,
    mlp_down,
    pre_gain,
    head_gain,
    codebook_table,
):
    tx = lax.axis_index("tx")
    ty = lax.axis_index("ty")
    core = ty % 2
    rows, width = hidden_in.shape
    full_width = width * 128
    half = rows // 2
    devices = 128

    both = hidden_in.reshape(devices, 2, 2, width)
    kept = jnp.where(core == 0, both[:, 0], both[:, 1]).reshape(half, width)
    given = jnp.where(core == 0, both[:, 1], both[:, 0]).reshape(half, width)
    gains = jnp.pad(jnp.stack([norm_gain, final_gain]), ((0, 14), (0, 0)))
    taken = swap(jnp.concatenate([given, gains]))
    residual = jnp.concatenate([kept, taken[:half]], axis=1).astype(F32)
    gain_in = jnp.concatenate([norm_gain, taken[half]]).astype(F32)
    gain_out = jnp.concatenate([final_gain, taken[half + 1]]).astype(F32)
    scaled = (residual * gain_in).astype(BF16)
    squares = split_sum(jnp.sum(residual * residual, axis=1))

    def relative(value):
        return [
            lax.dynamic_index_in_dim(value, tx ^ mask, 0, keepdims=False) for mask in (0,) + ORDER
        ]

    qkv_pair = jnp.stack([qkv_weight, swap(qkv_weight)])
    qkv_blocks = qkv_pair.reshape(2, 4, width, -1).transpose(1, 0, 2, 3)
    qkv_here = jnp.concatenate(relative(qkv_blocks)).reshape(8 * width, -1)
    gathered = jnp.concatenate(with_others(scaled), axis=1)
    partial_qkv = jnp.dot(gathered, qkv_here, preferred_element_type=F32).astype(BF16)
    sent = jnp.concatenate([partial_qkv, squares], axis=1).reshape(devices, 2, -1)
    got = lax.all_to_all(sent, ("ty", "tx"), 0, 0, tiled=True)
    sums = jnp.sum(got.reshape(16, 2, 4, 2, -1).astype(F32), axis=0)
    sums = sums.transpose(0, 2, 1, 3).reshape(16, -1)

    cosine, sine = rotation(lengths)
    (spread,) = call(
        functools.partial(attend_kernel, full_width),
        [((devices, 2, HEADS // 4 * HEAD_DIM), BF16)],
        sums,
        qkv_bias.astype(F32).reshape(-1, HEAD_DIM),
        cosine,
        sine,
        lengths[:, None],
        in_hbm(key_cache),
        in_hbm(value_cache),
        name="attend",
        specs=[VMEM] * 5 + [HBM] * 2,
        out_specs=[HBM],
        scratch=[
            pltpu.VMEM((4 * (HEADS + 2 * KV_HEADS), HEAD_DIM), F32),
            pltpu.VMEM((4 * HEADS, LMAX), F32),
            pltpu.VMEM((8, 2, HEADS // 4 * HEAD_DIM), BF16),
            pltpu.VMEM(key_cache.shape, BF16),
            pltpu.VMEM(value_cache.shape, BF16),
            pltpu.SemaphoreType.DMA((16,)),
        ],
    )
    spread = lax.all_to_all(spread, ("ty", "tx"), 0, 0, tiled=True).reshape(half, -1)
    out_pair = jnp.stack([out_weight, swap(out_weight)], axis=1)
    out_pair = out_pair.reshape(-1, 2, 4, width).transpose(2, 0, 1, 3)
    out_here = jnp.concatenate(relative(out_pair.reshape(4, -1, 2 * width)), axis=1)
    partial_out = jnp.dot(spread, out_here, preferred_element_type=F32).astype(BF16)
    pieces = jnp.split(partial_out, 4, axis=1)
    pieces = [pieces[0]] + [flip(piece, mask) for piece, mask in zip(pieces[1:], ORDER)]
    pieces = [piece.astype(F32) for piece in pieces]
    projected = (pieces[0] + pieces[3]) + (pieces[1] + pieces[2])
    leaving = (residual + projected).astype(BF16)
    other = swap(leaving[:, width:])

    in_blocks = relative(in_weight.reshape(4, width, -1))
    in_blocks = [in_blocks[0]] + [flip(b, mask) for b, mask in zip(in_blocks[1:], ORDER)]
    in_blocks = jnp.stack([in_blocks[((0,) + ORDER).index(mask)] for mask in range(4)])
    in_own = jnp.concatenate(
        [lax.dynamic_index_in_dim(in_blocks, tx ^ place, 0, keepdims=False) for place in range(4)],
        axis=1,
    )
    in_here = jnp.concatenate([in_own, swap(in_own)])
    exact = leaving.astype(F32)
    final_rows = (exact * gain_out).astype(BF16)
    final_squares = split_sum(jnp.sum(exact * exact, axis=1))
    partial_start = jnp.dot(final_rows, in_here, preferred_element_type=F32).astype(BF16)
    sent = jnp.concatenate([partial_start, final_squares], axis=1).reshape(32, 8, -1)
    got = lax.all_to_all(sent, "ty", 0, 0, tiled=True)
    (got,) = call(fold_kernel, [((16, sent.shape[2]), BF16)], got, name="fold")
    starts = with_others(got)
    depth_width = partial_start.shape[1]

    block_rows = got.shape[0]
    entries = codebook_table.shape[1]

    def by_core(value):
        return value.reshape(4, 2, 2, -1).transpose(1, 0, 2, 3).reshape(block_rows, -1)

    codes = lax.dynamic_slice_in_dim(codebook_ids, ty * block_rows, block_rows, 0)
    codes = by_core(codes) - tx * entries
    chosen = codes.T[: STEPS - 1, :, None] == jnp.arange(entries, dtype=jnp.int32)
    embeds = lax.dot_general(
        chosen.astype(BF16),
        codebook_table[: STEPS - 1],
        (((2,), (1,)), ((0,), (0,))),
        preferred_element_type=F32,
    ).astype(BF16)
    sides = jnp.split(embeds, 2, axis=2)
    sides = [side + flip(side, mask) for side, mask in zip(sides, (1, 3))]
    sides = [side + flip(side, mask) for side, mask in zip(sides, (3, 1))]
    owner_count = lax.axis_size("ty")
    block_owners = lax.dynamic_slice_in_dim(owners, ty * block_rows, block_rows, 0)
    same = block_owners[:, None] == block_owners[None, :]
    place = jnp.arange(block_rows)
    rank = jnp.sum((same & (place[None, :] < place[:, None])).astype(jnp.int32), axis=1)
    slots = by_core(block_owners * CAPACITY + rank)
    pre_gain = pre_gain.reshape(1, -1)
    head_gain = head_gain.reshape(1, -1)
    gate, up = load(mlp_gate, mlp_up, got)
    shape = (block_rows, depth_width)
    state, part, codes, slots, found, down = call(
        functools.partial(first_kernel, full_width),
        [
            (shape, F32),
            (shape, BF16),
            (codes.shape, jnp.int32),
            (slots.shape, jnp.int32),
            ((block_rows, 128), F32),
            pltpu.VMEM(mlp_down.shape, BF16),
        ],
        *starts,
        codes,
        slots,
        pre_gain,
        gate,
        up,
        in_hbm(mlp_down),
        name="depth_first",
        specs=[VMEM] * 9 + [HBM],
        scratch=[pltpu.SemaphoreType.DMA],
    )
    table_shape = codebook_table.shape[1:]
    for step in range(STEPS - 1):
        parts = with_others(part)
        state, part, outer = call(
            functools.partial(middle_kernel, step),
            [(shape, F32), (shape, BF16), (shape, BF16)],
            state,
            *parts,
            found,
            *sides,
            pre_gain,
            head_gain,
            gate,
            up,
            down,
            name="depth_step",
        )
        found, *extra = call(
            functools.partial(score_kernel if step else score_first_kernel, step),
            [(found.shape, F32)] + [pltpu.VMEM(table_shape, BF16)] * (step == 0),
            outer,
            codes,
            found,
            in_hbm(codebook_table),
            name="depth_score",
            specs=[VMEM] * 3 + [HBM],
            scratch=[pltpu.VMEM(table_shape, BF16), pltpu.SemaphoreType.DMA((2,))],
        )
        if step == 0:
            (last_table,) = extra
    parts = with_others(part)
    outgoing, other = call(
        functools.partial(last_kernel, STEPS - 1),
        [((owner_count, 4, 128), F32), (other.shape, BF16)],
        state,
        *parts,
        found,
        codes,
        slots,
        head_gain,
        last_table,
        other,
        name="depth_last",
    )

    incoming = lax.all_to_all(outgoing.reshape(devices, 128), ("ty", "tx"), 0, 0, tiled=True)
    other = other.reshape(devices, 1, 2, width)
    mine = leaving[:, :width].reshape(devices, 1, 2, width)
    hidden_out = jnp.where(
        core == 0,
        jnp.concatenate([mine, other], axis=1),
        jnp.concatenate([other, mine], axis=1),
    ).reshape(rows, width)
    incoming = jnp.sum(incoming.reshape(owner_count, 4, -1), axis=1)
    incoming = incoming[:, : 128 // 2].reshape(owner_count * CAPACITY, -1)
    logprob = incoming[:, STEPS : 2 * STEPS] - jnp.log(incoming[:, :STEPS])
    logprob = jnp.where(incoming[:, 2 * STEPS : 2 * STEPS + 1] > 0.0, logprob, 0.0)
    return (hidden_out, logprob.T[None])


def solution(mesh):
    placed = (
        P(None, ("ty", "tx")),
        P(("ty", "tx")),
        P("ty", "tx"),
        P(),
        P(("ty", "tx"), None, None),
        P(("ty", "tx"), None, None),
        P(("ty", "tx")),
        P("tx", "ty"),
        P(("ty", "tx")),
        P("ty", "tx"),
        P(),
        P(),
        P(None, "tx"),
        P(None, "tx"),
        P("tx", None),
        P(),
        P(),
        P(None, "tx", None),
    )
    return jax.shard_map(
        body,
        mesh=mesh,
        in_specs=placed,
        out_specs=(P(None, ("ty", "tx")), P("ty", None, None)),
        check_vma=False,
    )
```

```python
import functools

import jax
import jax.numpy as jnp
from jax import lax
from jax.experimental import pallas as pl
from jax.experimental.pallas import tpu as pltpu
from jax.sharding import PartitionSpec as P

HEADS = 64
KV_HEADS = 8
HEAD_DIM = 128
STEPS = 8
LMAX = 128
CAPACITY = 2
ORDER = (2, 3, 1)
BF16 = jnp.bfloat16
F32 = jnp.float32


epsilon = 1e-06
rope_base = 1000000.0
embed_gain = 16.0


def rotation(position):
    half_dim = HEAD_DIM // 2
    frequency = jnp.exp(
        -jnp.log(rope_base) * (2.0 * jnp.arange(half_dim, dtype=F32) / HEAD_DIM)
    )
    phase_angle = position.astype(F32)[:, None] * frequency[None, :]
    cosine = jnp.cos(phase_angle)
    sine = jnp.sin(phase_angle)
    return (
        jnp.concatenate([cosine, cosine], axis=1),
        jnp.concatenate([-sine, sine], axis=1),
    )


def attend_kernel(
    full_width, sums, bias, cosine, sine, lengths, keys, values,
    out, heads, scores, blocks, key_here, value_here, sems,
):
    copies = [
        pltpu.make_async_copy(keys, key_here, sems.at[0]),
        pltpu.make_async_copy(values, value_here, sems.at[1]),
    ]
    for copy in copies:
        copy.start()
    units = HEADS + 2 * KV_HEADS
    group = HEADS // KV_HEADS
    per_tx = units // 4
    width = per_tx * HEAD_DIM
    for core in range(2):
        block = sums[8 * core : 8 * core + 8, :]
        square = block[:, width : width + 1] + block[:, width + 1 : width + 2]
        first = jnp.sum(square[:4], axis=0, keepdims=True)
        second = jnp.sum(square[4:], axis=0, keepdims=True)
        place = lax.broadcasted_iota(jnp.int32, (8, 1), 0)
        scale = lax.rsqrt(jnp.where(place < 4, first, second) / full_width + epsilon)
        for unit in range(per_tx):
            piece = block[:, unit * HEAD_DIM : (unit + 1) * HEAD_DIM] * scale
            heads[pl.ds(2 * core * units + unit, 8, stride=per_tx), :] = piece
    queries = []
    owns = []
    news = []
    for row in range(4):
        raw = heads[row * units : (row + 1) * units, :].astype(BF16).astype(F32) + bias[...]
        turned = raw * cosine[row : row + 1, :] + pltpu.roll(raw, HEAD_DIM // 2, 1) * (
            sine[row : row + 1, :]
        )
        query = (turned[:HEADS] * HEAD_DIM ** (-0.5)).astype(BF16)
        new_key = turned[HEADS : HEADS + KV_HEADS].astype(BF16).astype(F32)
        new_value = raw[HEADS + KV_HEADS :].astype(BF16).astype(F32)
        spread_key = jnp.concatenate(
            [jnp.broadcast_to(new_key[h : h + 1], (group, HEAD_DIM)) for h in range(KV_HEADS)]
        )
        query = query.astype(F32)
        queries.append(query)
        owns.append(jnp.sum(query * spread_key, axis=1, keepdims=True))
        news.append(new_value)
    copies[0].wait()
    for row in range(4):
        for head in range(KV_HEADS):
            part = slice(head * group, (head + 1) * group)
            scores[row * HEADS + head * group : row * HEADS + (head + 1) * group, :] = (
                lax.dot_general(
                    queries[row][part].astype(BF16),
                    key_here[row, :, head * HEAD_DIM : (head + 1) * HEAD_DIM],
                    (((1,), (1,)), ((), ())),
                    preferred_element_type=F32,
                )
            )
    copies[1].wait()
    slot = lax.broadcasted_iota(jnp.int32, (HEADS, LMAX), 1)
    for row in range(4):
        rows = slice(row * HEADS, (row + 1) * HEADS)
        weights = jnp.where(slot < lengths[row : row + 1, :], jnp.exp(scores[rows, :]), 0.0)
        own_weight = jnp.exp(owns[row])
        denominator = jnp.sum(weights, axis=1, keepdims=True) + own_weight
        probability = (weights / denominator).astype(BF16).astype(F32)
        own_prob = (own_weight / denominator).astype(BF16).astype(F32)
        for head in range(KV_HEADS):
            part = slice(head * group, (head + 1) * group)
            blended = jnp.dot(
                probability[part].astype(BF16),
                value_here[row, :, head * HEAD_DIM : (head + 1) * HEAD_DIM],
                preferred_element_type=F32,
            )
            heads[row * HEADS + head * group : row * HEADS + (head + 1) * group, :] = (
                blended + own_prob[part] * news[row][head : head + 1]
            )
    for core in range(2):
        for head in range(HEADS):
            tx, place = divmod(head, HEADS // 4)
            both = heads[pl.ds(2 * core * HEADS + head, 2, stride=HEADS), :]
            blocks[4 * core + tx, :, place * HEAD_DIM : (place + 1) * HEAD_DIM] = both.astype(BF16)
    copies = [
        pltpu.make_async_copy(blocks, out.at[pl.ds(8 * chip, 8)], sems.at[chip])
        for chip in range(out.shape[0] // 8)
    ]
    for copy in copies:
        copy.start()
    for copy in copies:
        copy.wait()


def flip(value, mask):
    return lax.ppermute(value, "tx", [(i, i ^ mask) for i in range(4)])


def with_others(value):
    return [value] + [flip(value, mask) for mask in ORDER]


def swap(value):
    return lax.ppermute(value, "ty", [(i, i ^ 1) for i in range(32)])


def split_sum(values):
    high = values.astype(BF16)
    low = (values - high.astype(F32)).astype(BF16)
    return jnp.pad(jnp.stack([high, low], axis=-1), ((0, 0), (0, 126)))


def norm_rows(state, gain):
    mean_square = jnp.mean(state * state, axis=-1, keepdims=True)
    return (state * lax.rsqrt(mean_square + epsilon) * gain).astype(BF16)


def hidden(state, pre_gain, gate, up):
    inner = norm_rows(state, pre_gain[...].astype(F32))
    gate_part = jnp.dot(inner, gate[...], preferred_element_type=F32)
    up_part = jnp.dot(inner, up[...], preferred_element_type=F32)
    return (gate_part / (1.0 + jnp.exp(-gate_part)) * up_part).astype(BF16)


def mlp(state, pre_gain, gate, up, down):
    act = hidden(state, pre_gain, gate, up)
    return jnp.dot(act, down[...], preferred_element_type=F32).astype(BF16)


def total_of(parts):
    one, two, three, four = [part[...].astype(F32) for part in parts]
    return (one + four) + (two + three)


def load_kernel(gate, up, after, gate_out, up_out, sems):
    copies = [
        pltpu.make_async_copy(gate, gate_out, sems.at[0]),
        pltpu.make_async_copy(up, up_out, sems.at[1]),
    ]
    for copy in copies:
        copy.start()
    for copy in copies:
        copy.wait()


def in_hbm(value):
    return pltpu.with_memory_space_constraint(value, pltpu.HBM)


def load(gate, up, after):
    return pl.pallas_call(
        load_kernel,
        out_shape=[pltpu.VMEM(gate.shape, BF16), pltpu.VMEM(up.shape, BF16)],
        in_specs=[HBM] * 2 + [VMEM],
        out_specs=[VMEM] * 2,
        scratch_shapes=[pltpu.SemaphoreType.DMA((2,))],
        name="depth_weights",
        compiler_params=pltpu.CompilerParams(vmem_limit_bytes=2**20),
        cost_estimate=pl.CostEstimate(
            flops=0, transcendentals=0, bytes_accessed=4 * (gate.size + up.size)
        ),
    )(in_hbm(gate), in_hbm(up), after)


def fold_kernel(chips, out):
    count, rows, columns = chips.shape
    width = columns - 128
    halves = []
    for core in range(2):
        total = chips[core].astype(F32)
        for chip in range(1, count // 2):
            total = total + chips[2 * chip + core].astype(F32)
        halves.append(total)
    total = jnp.concatenate(halves, axis=0)
    out[:, :width] = total[:, :width].astype(BF16)
    square = total[:, width : width + 1] + total[:, width + 1 : width + 2]
    high = square.astype(BF16).astype(F32)
    lane = lax.broadcasted_iota(jnp.int32, (2 * rows, 128), 1)
    tail = jnp.where(lane == 0, high, jnp.where(lane == 1, square - high, 0.0))
    out[:, width:] = tail.astype(BF16)


def first_kernel(
    full_width, a, b, c, d, codes, slots, pre_gain, gate, up, down,
    state, part, codes_out, slots_out, found, down_out, sem,
):
    copy = pltpu.make_async_copy(down, down_out, sem)
    copy.start()
    total = total_of((a, b, c, d))
    width = state.shape[1]
    square = total[:, width : width + 1] + total[:, width + 1 : width + 2]
    start = total[:, :width] * lax.rsqrt(square / full_width + epsilon)
    start = start.astype(BF16).astype(F32)
    state[...] = start
    codes_out[...] = codes[...]
    slots_out[...] = slots[...]
    found[...] = jnp.zeros(found.shape, F32)
    act = hidden(start, pre_gain, gate, up)
    copy.wait()
    part[...] = jnp.dot(act, down_out[...], preferred_element_type=F32).astype(BF16)


def score(step, outer, codes, table, found):
    logits = lax.dot_general(
        outer, table, (((1,), (1,)), ((), ())), preferred_element_type=F32
    )
    entry = lax.broadcasted_iota(jnp.int32, logits.shape, 1)
    chosen = codes[:, step : step + 1] == entry
    picked = jnp.sum(jnp.where(chosen, logits, 0.0), axis=1, keepdims=True)
    exp_total = jnp.sum(jnp.exp(logits), axis=1, keepdims=True)
    lane = lax.broadcasted_iota(jnp.int32, found.shape, 1)
    kept = jnp.where(lane == step, exp_total, found[...])
    return jnp.where(lane == STEPS + step, picked, kept)


def score_kernel(step, outer, codes, found, table, out, entries, sem):
    copy = pltpu.make_async_copy(table.at[step], entries, sem.at[0])
    copy.start()
    copy.wait()
    out[...] = score(step, outer[...], codes, entries[...], found)


def score_first_kernel(step, outer, codes, found, table, out, last, entries, sem):
    copy = pltpu.make_async_copy(table.at[STEPS - 1], last, sem.at[1])
    copy.start()
    score_kernel(step, outer, codes, found, table, out, entries, sem)
    copy.wait()


def middle_kernel(
    step, state, a, b, c, d, found, left, right, pre_gain, head_gain, gate, up, down,
    after, part, outer,
):
    total = state[...] + total_of((a, b, c, d))
    outer[...] = norm_rows(total, head_gain[...].astype(F32))
    embed = jnp.concatenate([left[step], right[step]], axis=1)
    total = total + embed_gain * embed.astype(F32)
    after[...] = total
    part[...] = mlp(total, pre_gain, gate, up, down)


def last_kernel(step, state, a, b, c, d, found, codes, slots, head_gain, table, other, out, kept):
    total = state[...] + total_of((a, b, c, d))
    outer = norm_rows(total, head_gain[...].astype(F32))
    done = score(step, outer, codes, table[...], found)
    lane = lax.broadcasted_iota(jnp.int32, done.shape, 1)
    done = jnp.where(lane == 2 * STEPS, 1.0, done)
    done = done + pltpu.roll(done, 128 // 4, 1)
    owner_count = out.shape[0]
    shape = (owner_count, 128)
    lane = lax.broadcasted_iota(jnp.int32, shape, 1)
    target = CAPACITY * lax.broadcasted_iota(jnp.int32, shape, 0) + lane // (128 // 4)
    result = jnp.zeros(shape, F32)
    for row in range(state.shape[0]):
        result = result + jnp.where(target == slots[row : row + 1, :], done[row : row + 1], 0.0)
    out[...] = jnp.broadcast_to(result[:, None, :], out.shape)
    kept[...] = other[...]


VMEM = pl.BlockSpec(memory_space=pltpu.VMEM)
HBM = pl.BlockSpec(memory_space=pltpu.HBM)


def call(kernel, outs, *operands, name, specs=None, out_specs=None, scratch=()):
    size = sum(w.size for w in operands)
    return pl.pallas_call(
        kernel,
        out_shape=[jax.ShapeDtypeStruct(*out) if type(out) is tuple else out for out in outs],
        in_specs=specs or [VMEM] * len(operands),
        out_specs=out_specs or [VMEM] * len(outs),
        scratch_shapes=scratch,
        name=name,
        compiler_params=pltpu.CompilerParams(vmem_limit_bytes=8 * 2**20),
        cost_estimate=pl.CostEstimate(
            flops=32 * size, transcendentals=2**14, bytes_accessed=2 * size + 2**18
        ),
    )(*operands)


def body(
    hidden_in,
    norm_gain,
    qkv_weight,
    qkv_bias,
    key_cache,
    value_cache,
    lengths,
    out_weight,
    final_gain,
    in_weight,
    owners,
    codebook_ids,
    mlp_gate,
    mlp_up,
    mlp_down,
    pre_gain,
    head_gain,
    codebook_table,
):
    tx = lax.axis_index("tx")
    ty = lax.axis_index("ty")
    core = ty % 2
    rows, width = hidden_in.shape
    full_width = width * 128
    half = rows // 2
    devices = 128

    gained = (hidden_in.astype(F32) * norm_gain.astype(F32)).astype(BF16)
    both = jnp.concatenate([hidden_in, gained], axis=1).reshape(devices, 2, 2, 2 * width)
    kept = jnp.where(core == 0, both[:, 0], both[:, 1]).reshape(half, 2 * width)
    given = jnp.where(core == 0, both[:, 1], both[:, 0]).reshape(half, 2 * width)
    taken = swap(given)
    residual = jnp.concatenate([kept[:, :width], taken[:, :width]], axis=1).astype(F32)
    scaled = jnp.concatenate([kept[:, width:], taken[:, width:]], axis=1)
    gain_out = jnp.concatenate([final_gain, swap(final_gain)]).astype(F32)
    squares = split_sum(jnp.sum(residual * residual, axis=1))

    def relative(value):
        return [
            lax.dynamic_index_in_dim(value, tx ^ mask, 0, keepdims=False) for mask in (0,) + ORDER
        ]

    qkv_pair = jnp.stack([qkv_weight, swap(qkv_weight)])
    qkv_blocks = qkv_pair.reshape(2, 4, width, -1).transpose(1, 0, 2, 3)
    qkv_here = jnp.concatenate(relative(qkv_blocks)).reshape(8 * width, -1)
    gathered = jnp.concatenate(with_others(scaled), axis=1)
    partial_qkv = jnp.dot(gathered, qkv_here, preferred_element_type=F32).astype(BF16)
    sent = jnp.concatenate([partial_qkv, squares], axis=1).reshape(devices, 2, -1)
    got = lax.all_to_all(sent, ("ty", "tx"), 0, 0, tiled=True)
    sums = jnp.sum(got.reshape(16, 2, 4, 2, -1).astype(F32), axis=0)
    sums = sums.transpose(0, 2, 1, 3).reshape(16, -1)

    cosine, sine = rotation(lengths)
    (spread,) = call(
        functools.partial(attend_kernel, full_width),
        [((devices, 2, HEADS // 4 * HEAD_DIM), BF16)],
        sums,
        qkv_bias.astype(F32).reshape(-1, HEAD_DIM),
        cosine,
        sine,
        lengths[:, None],
        in_hbm(key_cache),
        in_hbm(value_cache),
        name="attend",
        specs=[VMEM] * 5 + [HBM] * 2,
        out_specs=[HBM],
        scratch=[
            pltpu.VMEM((4 * (HEADS + 2 * KV_HEADS), HEAD_DIM), F32),
            pltpu.VMEM((4 * HEADS, LMAX), F32),
            pltpu.VMEM((8, 2, HEADS // 4 * HEAD_DIM), BF16),
            pltpu.VMEM(key_cache.shape, BF16),
            pltpu.VMEM(value_cache.shape, BF16),
            pltpu.SemaphoreType.DMA((16,)),
        ],
    )
    spread = lax.all_to_all(spread, ("ty", "tx"), 0, 0, tiled=True).reshape(half, -1)
    out_pair = jnp.stack([out_weight, swap(out_weight)], axis=1)
    out_pair = out_pair.reshape(-1, 2, 4, width).transpose(2, 0, 1, 3)
    out_here = jnp.concatenate(relative(out_pair.reshape(4, -1, 2 * width)), axis=1)
    partial_out = jnp.dot(spread, out_here, preferred_element_type=F32).astype(BF16)
    pieces = jnp.split(partial_out, 4, axis=1)
    pieces = [pieces[0]] + [flip(piece, mask) for piece, mask in zip(pieces[1:], ORDER)]
    pieces = [piece.astype(F32) for piece in pieces]
    projected = (pieces[0] + pieces[3]) + (pieces[1] + pieces[2])
    leaving = (residual + projected).astype(BF16)
    other = swap(leaving[:, width:])

    in_blocks = relative(in_weight.reshape(4, width, -1))
    in_blocks = [in_blocks[0]] + [flip(b, mask) for b, mask in zip(in_blocks[1:], ORDER)]
    in_blocks = jnp.stack([in_blocks[((0,) + ORDER).index(mask)] for mask in range(4)])
    in_own = jnp.concatenate(
        [lax.dynamic_index_in_dim(in_blocks, tx ^ place, 0, keepdims=False) for place in range(4)],
        axis=1,
    )
    in_here = jnp.concatenate([in_own, swap(in_own)])
    exact = leaving.astype(F32)
    final_rows = (exact * gain_out).astype(BF16)
    final_squares = split_sum(jnp.sum(exact * exact, axis=1))
    partial_start = jnp.dot(final_rows, in_here, preferred_element_type=F32).astype(BF16)
    sent = jnp.concatenate([partial_start, final_squares], axis=1).reshape(32, 8, -1)
    got = lax.all_to_all(sent, "ty", 0, 0, tiled=True)
    (got,) = call(fold_kernel, [((16, sent.shape[2]), BF16)], got, name="fold")
    starts = with_others(got)
    depth_width = partial_start.shape[1]

    block_rows = got.shape[0]
    entries = codebook_table.shape[1]

    def by_core(value):
        return value.reshape(4, 2, 2, -1).transpose(1, 0, 2, 3).reshape(block_rows, -1)

    codes = lax.dynamic_slice_in_dim(codebook_ids, ty * block_rows, block_rows, 0)
    codes = by_core(codes) - tx * entries
    chosen = codes.T[: STEPS - 1, :, None] == jnp.arange(entries, dtype=jnp.int32)
    embeds = lax.dot_general(
        chosen.astype(BF16),
        codebook_table[: STEPS - 1],
        (((2,), (1,)), ((0,), (0,))),
        preferred_element_type=F32,
    ).astype(BF16)
    sides = jnp.split(embeds, 2, axis=2)
    sides = [side + flip(side, mask) for side, mask in zip(sides, (1, 3))]
    sides = [side + flip(side, mask) for side, mask in zip(sides, (3, 1))]
    owner_count = lax.axis_size("ty")
    block_owners = lax.dynamic_slice_in_dim(owners, ty * block_rows, block_rows, 0)
    same = block_owners[:, None] == block_owners[None, :]
    place = jnp.arange(block_rows)
    rank = jnp.sum((same & (place[None, :] < place[:, None])).astype(jnp.int32), axis=1)
    slots = by_core(block_owners * CAPACITY + rank)
    pre_gain = pre_gain.reshape(1, -1)
    head_gain = head_gain.reshape(1, -1)
    gate, up = load(mlp_gate, mlp_up, got)
    shape = (block_rows, depth_width)
    state, part, codes, slots, found, down = call(
        functools.partial(first_kernel, full_width),
        [
            (shape, F32),
            (shape, BF16),
            (codes.shape, jnp.int32),
            (slots.shape, jnp.int32),
            ((block_rows, 128), F32),
            pltpu.VMEM(mlp_down.shape, BF16),
        ],
        *starts,
        codes,
        slots,
        pre_gain,
        gate,
        up,
        in_hbm(mlp_down),
        name="depth_first",
        specs=[VMEM] * 9 + [HBM],
        scratch=[pltpu.SemaphoreType.DMA],
    )
    table_shape = codebook_table.shape[1:]
    for step in range(STEPS - 1):
        parts = with_others(part)
        state, part, outer = call(
            functools.partial(middle_kernel, step),
            [(shape, F32), (shape, BF16), (shape, BF16)],
            state,
            *parts,
            found,
            *sides,
            pre_gain,
            head_gain,
            gate,
            up,
            down,
            name="depth_step",
        )
        found, *extra = call(
            functools.partial(score_kernel if step else score_first_kernel, step),
            [(found.shape, F32)] + [pltpu.VMEM(table_shape, BF16)] * (step == 0),
            outer,
            codes,
            found,
            in_hbm(codebook_table),
            name="depth_score",
            specs=[VMEM] * 3 + [HBM],
            scratch=[pltpu.VMEM(table_shape, BF16), pltpu.SemaphoreType.DMA((2,))],
        )
        if step == 0:
            (last_table,) = extra
    parts = with_others(part)
    outgoing, other = call(
        functools.partial(last_kernel, STEPS - 1),
        [((owner_count, 4, 128), F32), (other.shape, BF16)],
        state,
        *parts,
        found,
        codes,
        slots,
        head_gain,
        last_table,
        other,
        name="depth_last",
    )

    incoming = lax.all_to_all(outgoing.reshape(devices, 128), ("ty", "tx"), 0, 0, tiled=True)
    other = other.reshape(devices, 1, 2, width)
    mine = leaving[:, :width].reshape(devices, 1, 2, width)
    hidden_out = jnp.where(
        core == 0,
        jnp.concatenate([mine, other], axis=1),
        jnp.concatenate([other, mine], axis=1),
    ).reshape(rows, width)
    incoming = jnp.sum(incoming.reshape(owner_count, 4, -1), axis=1)
    incoming = incoming[:, : 128 // 2].reshape(owner_count * CAPACITY, -1)
    logprob = incoming[:, STEPS : 2 * STEPS] - jnp.log(incoming[:, :STEPS])
    logprob = jnp.where(incoming[:, 2 * STEPS : 2 * STEPS + 1] > 0.0, logprob, 0.0)
    return (hidden_out, logprob.T[None])


def solution(mesh):
    placed = (
        P(None, ("ty", "tx")),
        P(("ty", "tx")),
        P("ty", "tx"),
        P(),
        P(("ty", "tx"), None, None),
        P(("ty", "tx"), None, None),
        P(("ty", "tx")),
        P("tx", "ty"),
        P(("ty", "tx")),
        P("ty", "tx"),
        P(),
        P(),
        P(None, "tx"),
        P(None, "tx"),
        P("tx", None),
        P(),
        P(),
        P(None, "tx", None),
    )
    return jax.shard_map(
        body,
        mesh=mesh,
        in_specs=placed,
        out_specs=(P(None, ("ty", "tx")), P("ty", None, None)),
        check_vma=False,
    )
```

```python
import functools

import jax
import jax.numpy as jnp
from jax import lax
from jax.experimental import pallas as pl
from jax.experimental.pallas import tpu as pltpu
from jax.sharding import PartitionSpec as P

HEADS = 64
KV_HEADS = 8
HEAD_DIM = 128
STEPS = 8
LMAX = 128
CAPACITY = 2
ORDER = (2, 3, 1)
BF16 = jnp.bfloat16
F32 = jnp.float32


epsilon = 1e-06
rope_base = 1000000.0
embed_gain = 16.0


def rotation(position):
    half_dim = HEAD_DIM // 2
    frequency = jnp.exp(
        -jnp.log(rope_base) * (2.0 * jnp.arange(half_dim, dtype=F32) / HEAD_DIM)
    )
    phase_angle = position.astype(F32)[:, None] * frequency[None, :]
    cosine = jnp.cos(phase_angle)
    sine = jnp.sin(phase_angle)
    return (
        jnp.concatenate([cosine, cosine], axis=1),
        jnp.concatenate([-sine, sine], axis=1),
    )


def attend_kernel(
    full_width, sums, bias, cosine, sine, lengths, keys, values,
    out, heads, scores, blocks, key_here, value_here, sems,
):
    copies = [
        pltpu.make_async_copy(keys, key_here, sems.at[0]),
        pltpu.make_async_copy(values, value_here, sems.at[1]),
    ]
    for copy in copies:
        copy.start()
    units = HEADS + 2 * KV_HEADS
    group = HEADS // KV_HEADS
    per_tx = units // 4
    width = per_tx * HEAD_DIM
    for core in range(2):
        block = sums[8 * core : 8 * core + 8, :]
        square = block[:, width : width + 1] + block[:, width + 1 : width + 2]
        first = jnp.sum(square[:4], axis=0, keepdims=True)
        second = jnp.sum(square[4:], axis=0, keepdims=True)
        place = lax.broadcasted_iota(jnp.int32, (8, 1), 0)
        scale = lax.rsqrt(jnp.where(place < 4, first, second) / full_width + epsilon)
        for unit in range(per_tx):
            piece = block[:, unit * HEAD_DIM : (unit + 1) * HEAD_DIM] * scale
            heads[pl.ds(2 * core * units + unit, 8, stride=per_tx), :] = piece
    queries = []
    owns = []
    news = []
    for row in range(4):
        raw = heads[row * units : (row + 1) * units, :].astype(BF16).astype(F32) + bias[...]
        turned = raw * cosine[row : row + 1, :] + pltpu.roll(raw, HEAD_DIM // 2, 1) * (
            sine[row : row + 1, :]
        )
        query = (turned[:HEADS] * HEAD_DIM ** (-0.5)).astype(BF16)
        new_key = turned[HEADS : HEADS + KV_HEADS].astype(BF16).astype(F32)
        new_value = raw[HEADS + KV_HEADS :].astype(BF16).astype(F32)
        spread_key = jnp.concatenate(
            [jnp.broadcast_to(new_key[h : h + 1], (group, HEAD_DIM)) for h in range(KV_HEADS)]
        )
        query = query.astype(F32)
        queries.append(query)
        owns.append(jnp.sum(query * spread_key, axis=1, keepdims=True))
        news.append(new_value)
    copies[0].wait()
    for row in range(4):
        for head in range(KV_HEADS):
            part = slice(head * group, (head + 1) * group)
            scores[row * HEADS + head * group : row * HEADS + (head + 1) * group, :] = (
                lax.dot_general(
                    queries[row][part].astype(BF16),
                    key_here[row, :, head * HEAD_DIM : (head + 1) * HEAD_DIM],
                    (((1,), (1,)), ((), ())),
                    preferred_element_type=F32,
                )
            )
    copies[1].wait()
    slot = lax.broadcasted_iota(jnp.int32, (HEADS, LMAX), 1)
    for row in range(4):
        rows = slice(row * HEADS, (row + 1) * HEADS)
        weights = jnp.where(slot < lengths[row : row + 1, :], jnp.exp(scores[rows, :]), 0.0)
        own_weight = jnp.exp(owns[row])
        denominator = jnp.sum(weights, axis=1, keepdims=True) + own_weight
        probability = (weights / denominator).astype(BF16).astype(F32)
        own_prob = (own_weight / denominator).astype(BF16).astype(F32)
        for head in range(KV_HEADS):
            part = slice(head * group, (head + 1) * group)
            blended = jnp.dot(
                probability[part].astype(BF16),
                value_here[row, :, head * HEAD_DIM : (head + 1) * HEAD_DIM],
                preferred_element_type=F32,
            )
            heads[row * HEADS + head * group : row * HEADS + (head + 1) * group, :] = (
                blended + own_prob[part] * news[row][head : head + 1]
            )
    for core in range(2):
        for head in range(HEADS):
            tx, place = divmod(head, HEADS // 4)
            both = heads[pl.ds(2 * core * HEADS + head, 2, stride=HEADS), :]
            blocks[4 * core + tx, :, place * HEAD_DIM : (place + 1) * HEAD_DIM] = both.astype(BF16)
    copies = [
        pltpu.make_async_copy(blocks, out.at[pl.ds(8 * chip, 8)], sems.at[chip])
        for chip in range(out.shape[0] // 8)
    ]
    for copy in copies:
        copy.start()
    for copy in copies:
        copy.wait()


def flip(value, mask):
    return lax.ppermute(value, "tx", [(i, i ^ mask) for i in range(4)])


def with_others(value):
    return [value] + [flip(value, mask) for mask in ORDER]


def swap(value):
    return lax.ppermute(value, "ty", [(i, i ^ 1) for i in range(32)])


def split_sum(values):
    high = values.astype(BF16)
    low = (values - high.astype(F32)).astype(BF16)
    return jnp.pad(jnp.stack([high, low], axis=-1), ((0, 0), (0, 126)))


def norm_rows(state, gain):
    mean_square = jnp.mean(state * state, axis=-1, keepdims=True)
    return (state * lax.rsqrt(mean_square + epsilon) * gain).astype(BF16)


def hidden(state, pre_gain, gate, up):
    inner = norm_rows(state, pre_gain[...].astype(F32))
    gate_part = jnp.dot(inner, gate[...], preferred_element_type=F32)
    up_part = jnp.dot(inner, up[...], preferred_element_type=F32)
    return (gate_part / (1.0 + jnp.exp(-gate_part)) * up_part).astype(BF16)


def mlp(state, pre_gain, gate, up, down):
    act = hidden(state, pre_gain, gate, up)
    return jnp.dot(act, down[...], preferred_element_type=F32).astype(BF16)


def total_of(parts):
    one, two, three, four = [part[...].astype(F32) for part in parts]
    return (one + four) + (two + three)


def load_kernel(gate, up, after, gate_out, up_out, sems):
    copies = [
        pltpu.make_async_copy(gate, gate_out, sems.at[0]),
        pltpu.make_async_copy(up, up_out, sems.at[1]),
    ]
    for copy in copies:
        copy.start()
    for copy in copies:
        copy.wait()


def in_hbm(value):
    return pltpu.with_memory_space_constraint(value, pltpu.HBM)


def load(gate, up, after):
    return pl.pallas_call(
        load_kernel,
        out_shape=[pltpu.VMEM(gate.shape, BF16), pltpu.VMEM(up.shape, BF16)],
        in_specs=[HBM] * 2 + [VMEM],
        out_specs=[VMEM] * 2,
        scratch_shapes=[pltpu.SemaphoreType.DMA((2,))],
        name="depth_weights",
        compiler_params=pltpu.CompilerParams(vmem_limit_bytes=2**20),
        cost_estimate=pl.CostEstimate(
            flops=0, transcendentals=0, bytes_accessed=4 * (gate.size + up.size)
        ),
    )(in_hbm(gate), in_hbm(up), after)


def split_kernel(core_ref, far_columns, far_gain, kept, given, columns, gain, lines, pairs, sems):
    copies = [
        pltpu.make_async_copy(far_columns, columns, sems.at[0]),
        pltpu.make_async_copy(far_gain, gain, sems.at[1]),
    ]
    for copy in copies:
        copy.start()
    for copy in copies:
        copy.wait()
    value = columns[...].astype(F32).T
    gained = (value * gain[...].astype(F32)).astype(BF16).astype(F32)
    lines[...] = jnp.concatenate([value, gained], axis=1)
    count = lines.shape[0] // 4
    rows = [lines[pl.ds(i, count, stride=4), :] for i in range(4)]
    for out, core in ((kept, 0), (given, 1)):
        for pair in range(2):
            mine = jnp.where(core_ref[0] == core, rows[pair], rows[2 + pair])
            pairs[pl.ds(pair, count, stride=2), :] = mine
        out[...] = pairs[...].astype(BF16)


def join_kernel(kept, taken, residual, scaled, squares):
    width = kept.shape[1] // 2
    own, other = kept[...].astype(F32), taken[...].astype(F32)
    value = jnp.concatenate([own[:, :width], other[:, :width]], axis=1)
    residual[...] = value
    scaled[...] = jnp.concatenate([own[:, width:], other[:, width:]], axis=1).astype(BF16)
    square = jnp.sum(value * value, axis=1, keepdims=True)
    high = square.astype(BF16).astype(F32)
    lane = lax.broadcasted_iota(jnp.int32, squares.shape, 1)
    tail = jnp.where(lane == 0, high, jnp.where(lane == 1, square - high, 0.0))
    squares[...] = tail.astype(BF16)


def fold_kernel(chips, out):
    count, rows, columns = chips.shape
    width = columns - 128
    halves = []
    for core in range(2):
        total = chips[core].astype(F32)
        for chip in range(1, count // 2):
            total = total + chips[2 * chip + core].astype(F32)
        halves.append(total)
    total = jnp.concatenate(halves, axis=0)
    out[:, :width] = total[:, :width].astype(BF16)
    square = total[:, width : width + 1] + total[:, width + 1 : width + 2]
    high = square.astype(BF16).astype(F32)
    lane = lax.broadcasted_iota(jnp.int32, (2 * rows, 128), 1)
    tail = jnp.where(lane == 0, high, jnp.where(lane == 1, square - high, 0.0))
    out[:, width:] = tail.astype(BF16)


def first_kernel(
    full_width, a, b, c, d, codes, slots, pre_gain, gate, up, down,
    state, part, codes_out, slots_out, found, down_out, sem,
):
    copy = pltpu.make_async_copy(down, down_out, sem)
    copy.start()
    total = total_of((a, b, c, d))
    width = state.shape[1]
    square = total[:, width : width + 1] + total[:, width + 1 : width + 2]
    start = total[:, :width] * lax.rsqrt(square / full_width + epsilon)
    start = start.astype(BF16).astype(F32)
    state[...] = start
    codes_out[...] = codes[...]
    slots_out[...] = slots[...]
    found[...] = jnp.zeros(found.shape, F32)
    act = hidden(start, pre_gain, gate, up)
    copy.wait()
    part[...] = jnp.dot(act, down_out[...], preferred_element_type=F32).astype(BF16)


def score(step, outer, codes, table, found):
    logits = lax.dot_general(
        outer, table, (((1,), (1,)), ((), ())), preferred_element_type=F32
    )
    entry = lax.broadcasted_iota(jnp.int32, logits.shape, 1)
    chosen = codes[:, step : step + 1] == entry
    picked = jnp.sum(jnp.where(chosen, logits, 0.0), axis=1, keepdims=True)
    exp_total = jnp.sum(jnp.exp(logits), axis=1, keepdims=True)
    lane = lax.broadcasted_iota(jnp.int32, found.shape, 1)
    kept = jnp.where(lane == step, exp_total, found[...])
    return jnp.where(lane == STEPS + step, picked, kept)


def score_kernel(step, outer, codes, found, table, out, entries, sem):
    copy = pltpu.make_async_copy(table.at[step], entries, sem.at[0])
    copy.start()
    copy.wait()
    out[...] = score(step, outer[...], codes, entries[...], found)


def score_first_kernel(step, outer, codes, found, table, out, last, entries, sem):
    copy = pltpu.make_async_copy(table.at[STEPS - 1], last, sem.at[1])
    copy.start()
    score_kernel(step, outer, codes, found, table, out, entries, sem)
    copy.wait()


def middle_kernel(
    step, state, a, b, c, d, found, left, right, pre_gain, head_gain, gate, up, down,
    after, part, outer,
):
    total = state[...] + total_of((a, b, c, d))
    outer[...] = norm_rows(total, head_gain[...].astype(F32))
    embed = jnp.concatenate([left[step], right[step]], axis=1)
    total = total + embed_gain * embed.astype(F32)
    after[...] = total
    part[...] = mlp(total, pre_gain, gate, up, down)


def last_kernel(step, state, a, b, c, d, found, codes, slots, head_gain, table, other, out, kept):
    total = state[...] + total_of((a, b, c, d))
    outer = norm_rows(total, head_gain[...].astype(F32))
    done = score(step, outer, codes, table[...], found)
    lane = lax.broadcasted_iota(jnp.int32, done.shape, 1)
    done = jnp.where(lane == 2 * STEPS, 1.0, done)
    done = done + pltpu.roll(done, 128 // 4, 1)
    owner_count = out.shape[0]
    shape = (owner_count, 128)
    lane = lax.broadcasted_iota(jnp.int32, shape, 1)
    target = CAPACITY * lax.broadcasted_iota(jnp.int32, shape, 0) + lane // (128 // 4)
    result = jnp.zeros(shape, F32)
    for row in range(state.shape[0]):
        result = result + jnp.where(target == slots[row : row + 1, :], done[row : row + 1], 0.0)
    out[...] = jnp.broadcast_to(result[:, None, :], out.shape)
    kept[...] = other[...]


VMEM = pl.BlockSpec(memory_space=pltpu.VMEM)
SMEM = pl.BlockSpec(memory_space=pltpu.SMEM)
HBM = pl.BlockSpec(memory_space=pltpu.HBM)


def call(kernel, outs, *operands, name, specs=None, out_specs=None, scratch=()):
    size = sum(w.size for w in operands)
    return pl.pallas_call(
        kernel,
        out_shape=[jax.ShapeDtypeStruct(*out) if type(out) is tuple else out for out in outs],
        in_specs=specs or [VMEM] * len(operands),
        out_specs=out_specs or [VMEM] * len(outs),
        scratch_shapes=scratch,
        name=name,
        compiler_params=pltpu.CompilerParams(vmem_limit_bytes=8 * 2**20),
        cost_estimate=pl.CostEstimate(
            flops=32 * size, transcendentals=2**14, bytes_accessed=2 * size + 2**18
        ),
    )(*operands)


def body(
    hidden_in,
    norm_gain,
    qkv_weight,
    qkv_bias,
    key_cache,
    value_cache,
    lengths,
    out_weight,
    final_gain,
    in_weight,
    owners,
    codebook_ids,
    mlp_gate,
    mlp_up,
    mlp_down,
    pre_gain,
    head_gain,
    codebook_table,
):
    tx = lax.axis_index("tx")
    ty = lax.axis_index("ty")
    core = ty % 2
    rows, width = hidden_in.shape
    full_width = width * 128
    half = rows // 2
    devices = 128

    kept, given = call(
        split_kernel,
        [((half, 2 * width), BF16)] * 2,
        core.reshape(1),
        in_hbm(hidden_in.T),
        in_hbm(norm_gain.reshape(1, -1)),
        name="split",
        specs=[SMEM, HBM, HBM],
        scratch=[
            pltpu.VMEM((width, rows), BF16),
            pltpu.VMEM((1, width), BF16),
            pltpu.VMEM((rows, 2 * width), F32),
            pltpu.VMEM((half, 2 * width), F32),
            pltpu.SemaphoreType.DMA((2,)),
        ],
    )
    residual, scaled, squares = call(
        join_kernel,
        [((half, 2 * width), F32), ((half, 2 * width), BF16), ((half, 128), BF16)],
        kept,
        swap(given),
        name="join",
    )
    gain_out = jnp.concatenate([final_gain, swap(final_gain)]).astype(F32)

    def relative(value):
        return [
            lax.dynamic_index_in_dim(value, tx ^ mask, 0, keepdims=False) for mask in (0,) + ORDER
        ]

    qkv_pair = jnp.stack([qkv_weight, swap(qkv_weight)])
    qkv_blocks = qkv_pair.reshape(2, 4, width, -1).transpose(1, 0, 2, 3)
    qkv_here = jnp.concatenate(relative(qkv_blocks)).reshape(8 * width, -1)
    gathered = jnp.concatenate(with_others(scaled), axis=1)
    partial_qkv = jnp.dot(gathered, qkv_here, preferred_element_type=F32).astype(BF16)
    sent = jnp.concatenate([partial_qkv, squares], axis=1).reshape(devices, 2, -1)
    got = lax.all_to_all(sent, ("ty", "tx"), 0, 0, tiled=True)
    sums = jnp.sum(got.reshape(16, 2, 4, 2, -1).astype(F32), axis=0)
    sums = sums.transpose(0, 2, 1, 3).reshape(16, -1)

    cosine, sine = rotation(lengths)
    (spread,) = call(
        functools.partial(attend_kernel, full_width),
        [((devices, 2, HEADS // 4 * HEAD_DIM), BF16)],
        sums,
        qkv_bias.astype(F32).reshape(-1, HEAD_DIM),
        cosine,
        sine,
        lengths[:, None],
        in_hbm(key_cache),
        in_hbm(value_cache),
        name="attend",
        specs=[VMEM] * 5 + [HBM] * 2,
        out_specs=[HBM],
        scratch=[
            pltpu.VMEM((4 * (HEADS + 2 * KV_HEADS), HEAD_DIM), F32),
            pltpu.VMEM((4 * HEADS, LMAX), F32),
            pltpu.VMEM((8, 2, HEADS // 4 * HEAD_DIM), BF16),
            pltpu.VMEM(key_cache.shape, BF16),
            pltpu.VMEM(value_cache.shape, BF16),
            pltpu.SemaphoreType.DMA((16,)),
        ],
    )
    spread = lax.all_to_all(spread, ("ty", "tx"), 0, 0, tiled=True).reshape(half, -1)
    out_pair = jnp.stack([out_weight, swap(out_weight)], axis=1)
    out_pair = out_pair.reshape(-1, 2, 4, width).transpose(2, 0, 1, 3)
    out_here = jnp.concatenate(relative(out_pair.reshape(4, -1, 2 * width)), axis=1)
    partial_out = jnp.dot(spread, out_here, preferred_element_type=F32).astype(BF16)
    pieces = jnp.split(partial_out, 4, axis=1)
    pieces = [pieces[0]] + [flip(piece, mask) for piece, mask in zip(pieces[1:], ORDER)]
    pieces = [piece.astype(F32) for piece in pieces]
    projected = (pieces[0] + pieces[3]) + (pieces[1] + pieces[2])
    leaving = (residual + projected).astype(BF16)
    other = swap(leaving[:, width:])

    in_blocks = relative(in_weight.reshape(4, width, -1))
    in_blocks = [in_blocks[0]] + [flip(b, mask) for b, mask in zip(in_blocks[1:], ORDER)]
    in_blocks = jnp.stack([in_blocks[((0,) + ORDER).index(mask)] for mask in range(4)])
    in_own = jnp.concatenate(
        [lax.dynamic_index_in_dim(in_blocks, tx ^ place, 0, keepdims=False) for place in range(4)],
        axis=1,
    )
    in_here = jnp.concatenate([in_own, swap(in_own)])
    exact = leaving.astype(F32)
    final_rows = (exact * gain_out).astype(BF16)
    final_squares = split_sum(jnp.sum(exact * exact, axis=1))
    partial_start = jnp.dot(final_rows, in_here, preferred_element_type=F32).astype(BF16)
    sent = jnp.concatenate([partial_start, final_squares], axis=1).reshape(32, 8, -1)
    got = lax.all_to_all(sent, "ty", 0, 0, tiled=True)
    (got,) = call(fold_kernel, [((16, sent.shape[2]), BF16)], got, name="fold")
    starts = with_others(got)
    depth_width = partial_start.shape[1]

    block_rows = got.shape[0]
    entries = codebook_table.shape[1]

    def by_core(value):
        return value.reshape(4, 2, 2, -1).transpose(1, 0, 2, 3).reshape(block_rows, -1)

    codes = lax.dynamic_slice_in_dim(codebook_ids, ty * block_rows, block_rows, 0)
    codes = by_core(codes) - tx * entries
    chosen = codes.T[: STEPS - 1, :, None] == jnp.arange(entries, dtype=jnp.int32)
    embeds = lax.dot_general(
        chosen.astype(BF16),
        codebook_table[: STEPS - 1],
        (((2,), (1,)), ((0,), (0,))),
        preferred_element_type=F32,
    ).astype(BF16)
    sides = jnp.split(embeds, 2, axis=2)
    sides = [side + flip(side, mask) for side, mask in zip(sides, (1, 3))]
    sides = [side + flip(side, mask) for side, mask in zip(sides, (3, 1))]
    owner_count = lax.axis_size("ty")
    block_owners = lax.dynamic_slice_in_dim(owners, ty * block_rows, block_rows, 0)
    same = block_owners[:, None] == block_owners[None, :]
    place = jnp.arange(block_rows)
    rank = jnp.sum((same & (place[None, :] < place[:, None])).astype(jnp.int32), axis=1)
    slots = by_core(block_owners * CAPACITY + rank)
    pre_gain = pre_gain.reshape(1, -1)
    head_gain = head_gain.reshape(1, -1)
    gate, up = load(mlp_gate, mlp_up, got)
    shape = (block_rows, depth_width)
    state, part, codes, slots, found, down = call(
        functools.partial(first_kernel, full_width),
        [
            (shape, F32),
            (shape, BF16),
            (codes.shape, jnp.int32),
            (slots.shape, jnp.int32),
            ((block_rows, 128), F32),
            pltpu.VMEM(mlp_down.shape, BF16),
        ],
        *starts,
        codes,
        slots,
        pre_gain,
        gate,
        up,
        in_hbm(mlp_down),
        name="depth_first",
        specs=[VMEM] * 9 + [HBM],
        scratch=[pltpu.SemaphoreType.DMA],
    )
    table_shape = codebook_table.shape[1:]
    for step in range(STEPS - 1):
        parts = with_others(part)
        state, part, outer = call(
            functools.partial(middle_kernel, step),
            [(shape, F32), (shape, BF16), (shape, BF16)],
            state,
            *parts,
            found,
            *sides,
            pre_gain,
            head_gain,
            gate,
            up,
            down,
            name="depth_step",
        )
        found, *extra = call(
            functools.partial(score_kernel if step else score_first_kernel, step),
            [(found.shape, F32)] + [pltpu.VMEM(table_shape, BF16)] * (step == 0),
            outer,
            codes,
            found,
            in_hbm(codebook_table),
            name="depth_score",
            specs=[VMEM] * 3 + [HBM],
            scratch=[pltpu.VMEM(table_shape, BF16), pltpu.SemaphoreType.DMA((2,))],
        )
        if step == 0:
            (last_table,) = extra
    parts = with_others(part)
    outgoing, other = call(
        functools.partial(last_kernel, STEPS - 1),
        [((owner_count, 4, 128), F32), (other.shape, BF16)],
        state,
        *parts,
        found,
        codes,
        slots,
        head_gain,
        last_table,
        other,
        name="depth_last",
    )

    incoming = lax.all_to_all(outgoing.reshape(devices, 128), ("ty", "tx"), 0, 0, tiled=True)
    other = other.reshape(devices, 1, 2, width)
    mine = leaving[:, :width].reshape(devices, 1, 2, width)
    hidden_out = jnp.where(
        core == 0,
        jnp.concatenate([mine, other], axis=1),
        jnp.concatenate([other, mine], axis=1),
    ).reshape(rows, width)
    incoming = jnp.sum(incoming.reshape(owner_count, 4, -1), axis=1)
    incoming = incoming[:, : 128 // 2].reshape(owner_count * CAPACITY, -1)
    logprob = incoming[:, STEPS : 2 * STEPS] - jnp.log(incoming[:, :STEPS])
    logprob = jnp.where(incoming[:, 2 * STEPS : 2 * STEPS + 1] > 0.0, logprob, 0.0)
    return (hidden_out, logprob.T[None])


def solution(mesh):
    placed = (
        P(None, ("ty", "tx")),
        P(("ty", "tx")),
        P("ty", "tx"),
        P(),
        P(("ty", "tx"), None, None),
        P(("ty", "tx"), None, None),
        P(("ty", "tx")),
        P("tx", "ty"),
        P(("ty", "tx")),
        P("ty", "tx"),
        P(),
        P(),
        P(None, "tx"),
        P(None, "tx"),
        P("tx", None),
        P(),
        P(),
        P(None, "tx", None),
    )
    return jax.shard_map(
        body,
        mesh=mesh,
        in_specs=placed,
        out_specs=(P(None, ("ty", "tx")), P("ty", None, None)),
        check_vma=False,
    )
```

```python
import functools

import jax
import jax.numpy as jnp
from jax import lax
from jax.experimental import pallas as pl
from jax.experimental.pallas import tpu as pltpu
from jax.sharding import PartitionSpec as P

HEADS = 64
KV_HEADS = 8
HEAD_DIM = 128
STEPS = 8
LMAX = 128
CAPACITY = 2
ORDER = (2, 3, 1)
BF16 = jnp.bfloat16
F32 = jnp.float32


epsilon = 1e-06
rope_base = 1000000.0
embed_gain = 16.0


def rotation(position):
    half_dim = HEAD_DIM // 2
    frequency = jnp.exp(
        -jnp.log(rope_base) * (2.0 * jnp.arange(half_dim, dtype=F32) / HEAD_DIM)
    )
    phase_angle = position.astype(F32)[:, None] * frequency[None, :]
    cosine = jnp.cos(phase_angle)
    sine = jnp.sin(phase_angle)
    return (
        jnp.concatenate([cosine, cosine], axis=1),
        jnp.concatenate([-sine, sine], axis=1),
    )


def attend_kernel(
    full_width, sums, bias, cosine, sine, lengths, keys, values,
    out, heads, scores, blocks, key_here, value_here, sems,
):
    copies = [
        pltpu.make_async_copy(keys, key_here, sems.at[0]),
        pltpu.make_async_copy(values, value_here, sems.at[1]),
    ]
    for copy in copies:
        copy.start()
    units = HEADS + 2 * KV_HEADS
    group = HEADS // KV_HEADS
    per_tx = units // 4
    width = per_tx * HEAD_DIM
    for core in range(2):
        block = sums[8 * core : 8 * core + 8, :]
        square = block[:, width : width + 1] + block[:, width + 1 : width + 2]
        first = jnp.sum(square[:4], axis=0, keepdims=True)
        second = jnp.sum(square[4:], axis=0, keepdims=True)
        place = lax.broadcasted_iota(jnp.int32, (8, 1), 0)
        scale = lax.rsqrt(jnp.where(place < 4, first, second) / full_width + epsilon)
        for unit in range(per_tx):
            piece = block[:, unit * HEAD_DIM : (unit + 1) * HEAD_DIM] * scale
            heads[pl.ds(2 * core * units + unit, 8, stride=per_tx), :] = piece
    queries = []
    owns = []
    news = []
    for row in range(4):
        raw = heads[row * units : (row + 1) * units, :].astype(BF16).astype(F32) + bias[...]
        turned = raw * cosine[row : row + 1, :] + pltpu.roll(raw, HEAD_DIM // 2, 1) * (
            sine[row : row + 1, :]
        )
        query = (turned[:HEADS] * HEAD_DIM ** (-0.5)).astype(BF16)
        new_key = turned[HEADS : HEADS + KV_HEADS].astype(BF16).astype(F32)
        new_value = raw[HEADS + KV_HEADS :].astype(BF16).astype(F32)
        spread_key = jnp.concatenate(
            [jnp.broadcast_to(new_key[h : h + 1], (group, HEAD_DIM)) for h in range(KV_HEADS)]
        )
        query = query.astype(F32)
        queries.append(query)
        owns.append(jnp.sum(query * spread_key, axis=1, keepdims=True))
        news.append(new_value)
    copies[0].wait()
    for row in range(4):
        for head in range(KV_HEADS):
            part = slice(head * group, (head + 1) * group)
            scores[row * HEADS + head * group : row * HEADS + (head + 1) * group, :] = (
                lax.dot_general(
                    queries[row][part].astype(BF16),
                    key_here[row, :, head * HEAD_DIM : (head + 1) * HEAD_DIM],
                    (((1,), (1,)), ((), ())),
                    preferred_element_type=F32,
                )
            )
    copies[1].wait()
    slot = lax.broadcasted_iota(jnp.int32, (HEADS, LMAX), 1)
    for row in range(4):
        rows = slice(row * HEADS, (row + 1) * HEADS)
        weights = jnp.where(slot < lengths[row : row + 1, :], jnp.exp(scores[rows, :]), 0.0)
        own_weight = jnp.exp(owns[row])
        denominator = jnp.sum(weights, axis=1, keepdims=True) + own_weight
        probability = (weights / denominator).astype(BF16).astype(F32)
        own_prob = (own_weight / denominator).astype(BF16).astype(F32)
        for head in range(KV_HEADS):
            part = slice(head * group, (head + 1) * group)
            blended = jnp.dot(
                probability[part].astype(BF16),
                value_here[row, :, head * HEAD_DIM : (head + 1) * HEAD_DIM],
                preferred_element_type=F32,
            )
            heads[row * HEADS + head * group : row * HEADS + (head + 1) * group, :] = (
                blended + own_prob[part] * news[row][head : head + 1]
            )
    for core in range(2):
        for head in range(HEADS):
            tx, place = divmod(head, HEADS // 4)
            both = heads[pl.ds(2 * core * HEADS + head, 2, stride=HEADS), :]
            blocks[4 * core + tx, :, place * HEAD_DIM : (place + 1) * HEAD_DIM] = both.astype(BF16)
    copies = [
        pltpu.make_async_copy(blocks, out.at[pl.ds(8 * chip, 8)], sems.at[chip])
        for chip in range(out.shape[0] // 8)
    ]
    for copy in copies:
        copy.start()
    for copy in copies:
        copy.wait()


def flip(value, mask):
    return lax.ppermute(value, "tx", [(i, i ^ mask) for i in range(4)])


def with_others(value):
    return [value] + [flip(value, mask) for mask in ORDER]


def swap(value):
    return lax.ppermute(value, "ty", [(i, i ^ 1) for i in range(32)])


def split_sum(values):
    high = values.astype(BF16)
    low = (values - high.astype(F32)).astype(BF16)
    return jnp.pad(jnp.stack([high, low], axis=-1), ((0, 0), (0, 126)))


def norm_rows(state, gain):
    mean_square = jnp.mean(state * state, axis=-1, keepdims=True)
    return (state * lax.rsqrt(mean_square + epsilon) * gain).astype(BF16)


def hidden(state, pre_gain, gate, up):
    inner = norm_rows(state, pre_gain[...].astype(F32))
    gate_part = jnp.dot(inner, gate[...], preferred_element_type=F32)
    up_part = jnp.dot(inner, up[...], preferred_element_type=F32)
    return (gate_part / (1.0 + jnp.exp(-gate_part)) * up_part).astype(BF16)


def mlp(state, pre_gain, gate, up, down):
    act = hidden(state, pre_gain, gate, up)
    return jnp.dot(act, down[...], preferred_element_type=F32).astype(BF16)


def total_of(parts):
    one, two, three, four = [part[...].astype(F32) for part in parts]
    return (one + four) + (two + three)


def in_parts(source, target, sems, first, count):
    rows = source.shape[0] // count
    copies = []
    for i in range(count):
        at = pl.ds(i * rows, rows)
        copies.append(pltpu.make_async_copy(source.at[at], target.at[at], sems.at[first + i]))
        copies[-1].start()
    return copies


def load_kernel(gate, up, after, gate_out, up_out, sems):
    copies = in_parts(gate, gate_out, sems, 0, 4) + in_parts(up, up_out, sems, 4, 4)
    for copy in copies:
        copy.wait()


def in_hbm(value):
    return pltpu.with_memory_space_constraint(value, pltpu.HBM)


def load(gate, up, after):
    return pl.pallas_call(
        load_kernel,
        out_shape=[pltpu.VMEM(gate.shape, BF16), pltpu.VMEM(up.shape, BF16)],
        in_specs=[HBM] * 2 + [VMEM],
        out_specs=[VMEM] * 2,
        scratch_shapes=[pltpu.SemaphoreType.DMA((8,))],
        name="depth_weights",
        compiler_params=pltpu.CompilerParams(vmem_limit_bytes=2**20),
        cost_estimate=pl.CostEstimate(
            flops=0, transcendentals=0, bytes_accessed=4 * (gate.size + up.size)
        ),
    )(in_hbm(gate), in_hbm(up), after)


def split_kernel(core_ref, far_columns, far_gain, kept, given, columns, gain, lines, pairs, sems):
    copies = [
        pltpu.make_async_copy(far_columns, columns, sems.at[0]),
        pltpu.make_async_copy(far_gain, gain, sems.at[1]),
    ]
    for copy in copies:
        copy.start()
    for copy in copies:
        copy.wait()
    value = columns[...].astype(F32).T
    gained = (value * gain[...].astype(F32)).astype(BF16).astype(F32)
    lines[...] = jnp.concatenate([value, gained], axis=1)
    count = lines.shape[0] // 4
    rows = [lines[pl.ds(i, count, stride=4), :] for i in range(4)]
    for out, core in ((kept, 0), (given, 1)):
        for pair in range(2):
            mine = jnp.where(core_ref[0] == core, rows[pair], rows[2 + pair])
            pairs[pl.ds(pair, count, stride=2), :] = mine
        out[...] = pairs[...].astype(BF16)


def join_kernel(kept, taken, residual, scaled, squares):
    width = kept.shape[1] // 2
    own, other = kept[...].astype(F32), taken[...].astype(F32)
    value = jnp.concatenate([own[:, :width], other[:, :width]], axis=1)
    residual[...] = value
    scaled[...] = jnp.concatenate([own[:, width:], other[:, width:]], axis=1).astype(BF16)
    square = jnp.sum(value * value, axis=1, keepdims=True)
    high = square.astype(BF16).astype(F32)
    lane = lax.broadcasted_iota(jnp.int32, squares.shape, 1)
    tail = jnp.where(lane == 0, high, jnp.where(lane == 1, square - high, 0.0))
    squares[...] = tail.astype(BF16)


def fold_kernel(chips, out):
    count, rows, columns = chips.shape
    width = columns - 128
    halves = []
    for core in range(2):
        total = chips[core].astype(F32)
        for chip in range(1, count // 2):
            total = total + chips[2 * chip + core].astype(F32)
        halves.append(total)
    total = jnp.concatenate(halves, axis=0)
    out[:, :width] = total[:, :width].astype(BF16)
    square = total[:, width : width + 1] + total[:, width + 1 : width + 2]
    high = square.astype(BF16).astype(F32)
    lane = lax.broadcasted_iota(jnp.int32, (2 * rows, 128), 1)
    tail = jnp.where(lane == 0, high, jnp.where(lane == 1, square - high, 0.0))
    out[:, width:] = tail.astype(BF16)


def first_kernel(
    full_width, a, b, c, d, codes, slots, pre_gain, gate, up, down,
    state, part, codes_out, slots_out, found, down_out, sems,
):
    copies = in_parts(down, down_out, sems, 0, 4)
    total = total_of((a, b, c, d))
    width = state.shape[1]
    square = total[:, width : width + 1] + total[:, width + 1 : width + 2]
    start = total[:, :width] * lax.rsqrt(square / full_width + epsilon)
    start = start.astype(BF16).astype(F32)
    state[...] = start
    codes_out[...] = codes[...]
    slots_out[...] = slots[...]
    found[...] = jnp.zeros(found.shape, F32)
    act = hidden(start, pre_gain, gate, up)
    for copy in copies:
        copy.wait()
    part[...] = jnp.dot(act, down_out[...], preferred_element_type=F32).astype(BF16)


def score(step, outer, codes, table, found):
    logits = lax.dot_general(
        outer, table, (((1,), (1,)), ((), ())), preferred_element_type=F32
    )
    entry = lax.broadcasted_iota(jnp.int32, logits.shape, 1)
    chosen = codes[:, step : step + 1] == entry
    picked = jnp.sum(jnp.where(chosen, logits, 0.0), axis=1, keepdims=True)
    exp_total = jnp.sum(jnp.exp(logits), axis=1, keepdims=True)
    lane = lax.broadcasted_iota(jnp.int32, found.shape, 1)
    kept = jnp.where(lane == step, exp_total, found[...])
    return jnp.where(lane == STEPS + step, picked, kept)


def score_kernel(step, outer, codes, found, table, out, entries, sem):
    copy = pltpu.make_async_copy(table.at[step], entries, sem.at[0])
    copy.start()
    copy.wait()
    out[...] = score(step, outer[...], codes, entries[...], found)


def score_first_kernel(step, outer, codes, found, table, out, last, entries, sem):
    copy = pltpu.make_async_copy(table.at[STEPS - 1], last, sem.at[1])
    copy.start()
    score_kernel(step, outer, codes, found, table, out, entries, sem)
    copy.wait()


def middle_kernel(
    step, state, a, b, c, d, found, left, right, pre_gain, head_gain, gate, up, down,
    after, part, outer,
):
    total = state[...] + total_of((a, b, c, d))
    outer[...] = norm_rows(total, head_gain[...].astype(F32))
    embed = jnp.concatenate([left[step], right[step]], axis=1)
    total = total + embed_gain * embed.astype(F32)
    after[...] = total
    part[...] = mlp(total, pre_gain, gate, up, down)


def last_kernel(step, state, a, b, c, d, found, codes, slots, head_gain, table, other, out, kept):
    total = state[...] + total_of((a, b, c, d))
    outer = norm_rows(total, head_gain[...].astype(F32))
    done = score(step, outer, codes, table[...], found)
    lane = lax.broadcasted_iota(jnp.int32, done.shape, 1)
    done = jnp.where(lane == 2 * STEPS, 1.0, done)
    done = done + pltpu.roll(done, 128 // 4, 1)
    owner_count = out.shape[0]
    shape = (owner_count, 128)
    lane = lax.broadcasted_iota(jnp.int32, shape, 1)
    target = CAPACITY * lax.broadcasted_iota(jnp.int32, shape, 0) + lane // (128 // 4)
    result = jnp.zeros(shape, F32)
    for row in range(state.shape[0]):
        result = result + jnp.where(target == slots[row : row + 1, :], done[row : row + 1], 0.0)
    out[...] = jnp.broadcast_to(result[:, None, :], out.shape)
    kept[...] = other[...]


VMEM = pl.BlockSpec(memory_space=pltpu.VMEM)
SMEM = pl.BlockSpec(memory_space=pltpu.SMEM)
HBM = pl.BlockSpec(memory_space=pltpu.HBM)


def call(kernel, outs, *operands, name, specs=None, out_specs=None, scratch=()):
    size = sum(w.size for w in operands)
    return pl.pallas_call(
        kernel,
        out_shape=[jax.ShapeDtypeStruct(*out) if type(out) is tuple else out for out in outs],
        in_specs=specs or [VMEM] * len(operands),
        out_specs=out_specs or [VMEM] * len(outs),
        scratch_shapes=scratch,
        name=name,
        compiler_params=pltpu.CompilerParams(vmem_limit_bytes=8 * 2**20),
        cost_estimate=pl.CostEstimate(
            flops=32 * size, transcendentals=2**14, bytes_accessed=2 * size + 2**18
        ),
    )(*operands)


def body(
    hidden_in,
    norm_gain,
    qkv_weight,
    qkv_bias,
    key_cache,
    value_cache,
    lengths,
    out_weight,
    final_gain,
    in_weight,
    owners,
    codebook_ids,
    mlp_gate,
    mlp_up,
    mlp_down,
    pre_gain,
    head_gain,
    codebook_table,
):
    tx = lax.axis_index("tx")
    ty = lax.axis_index("ty")
    core = ty % 2
    rows, width = hidden_in.shape
    full_width = width * 128
    half = rows // 2
    devices = 128

    kept, given = call(
        split_kernel,
        [((half, 2 * width), BF16)] * 2,
        core.reshape(1),
        in_hbm(hidden_in.T),
        in_hbm(norm_gain.reshape(1, -1)),
        name="split",
        specs=[SMEM, HBM, HBM],
        scratch=[
            pltpu.VMEM((width, rows), BF16),
            pltpu.VMEM((1, width), BF16),
            pltpu.VMEM((rows, 2 * width), F32),
            pltpu.VMEM((half, 2 * width), F32),
            pltpu.SemaphoreType.DMA((2,)),
        ],
    )
    residual, scaled, squares = call(
        join_kernel,
        [((half, 2 * width), F32), ((half, 2 * width), BF16), ((half, 128), BF16)],
        kept,
        swap(given),
        name="join",
    )
    gain_out = jnp.concatenate([final_gain, swap(final_gain)]).astype(F32)

    def relative(value):
        return [
            lax.dynamic_index_in_dim(value, tx ^ mask, 0, keepdims=False) for mask in (0,) + ORDER
        ]

    qkv_pair = jnp.stack([qkv_weight, swap(qkv_weight)])
    qkv_blocks = qkv_pair.reshape(2, 4, width, -1).transpose(1, 0, 2, 3)
    qkv_here = jnp.concatenate(relative(qkv_blocks)).reshape(8 * width, -1)
    gathered = jnp.concatenate(with_others(scaled), axis=1)
    partial_qkv = jnp.dot(gathered, qkv_here, preferred_element_type=F32).astype(BF16)
    sent = jnp.concatenate([partial_qkv, squares], axis=1).reshape(devices, 2, -1)
    got = lax.all_to_all(sent, ("ty", "tx"), 0, 0, tiled=True)
    sums = jnp.sum(got.reshape(16, 2, 4, 2, -1).astype(F32), axis=0)
    sums = sums.transpose(0, 2, 1, 3).reshape(16, -1)

    cosine, sine = rotation(lengths)
    (spread,) = call(
        functools.partial(attend_kernel, full_width),
        [((devices, 2, HEADS // 4 * HEAD_DIM), BF16)],
        sums,
        qkv_bias.astype(F32).reshape(-1, HEAD_DIM),
        cosine,
        sine,
        lengths[:, None],
        in_hbm(key_cache),
        in_hbm(value_cache),
        name="attend",
        specs=[VMEM] * 5 + [HBM] * 2,
        out_specs=[HBM],
        scratch=[
            pltpu.VMEM((4 * (HEADS + 2 * KV_HEADS), HEAD_DIM), F32),
            pltpu.VMEM((4 * HEADS, LMAX), F32),
            pltpu.VMEM((8, 2, HEADS // 4 * HEAD_DIM), BF16),
            pltpu.VMEM(key_cache.shape, BF16),
            pltpu.VMEM(value_cache.shape, BF16),
            pltpu.SemaphoreType.DMA((16,)),
        ],
    )
    spread = lax.all_to_all(spread, ("ty", "tx"), 0, 0, tiled=True).reshape(half, -1)
    out_pair = jnp.stack([out_weight, swap(out_weight)], axis=1)
    out_pair = out_pair.reshape(-1, 2, 4, width).transpose(2, 0, 1, 3)
    out_here = jnp.concatenate(relative(out_pair.reshape(4, -1, 2 * width)), axis=1)
    partial_out = jnp.dot(spread, out_here, preferred_element_type=F32).astype(BF16)
    pieces = jnp.split(partial_out, 4, axis=1)
    pieces = [pieces[0]] + [flip(piece, mask) for piece, mask in zip(pieces[1:], ORDER)]
    pieces = [piece.astype(F32) for piece in pieces]
    projected = (pieces[0] + pieces[3]) + (pieces[1] + pieces[2])
    leaving = (residual + projected).astype(BF16)
    other = swap(leaving[:, width:])

    in_blocks = relative(in_weight.reshape(4, width, -1))
    in_blocks = [in_blocks[0]] + [flip(b, mask) for b, mask in zip(in_blocks[1:], ORDER)]
    in_blocks = jnp.stack([in_blocks[((0,) + ORDER).index(mask)] for mask in range(4)])
    in_own = jnp.concatenate(
        [lax.dynamic_index_in_dim(in_blocks, tx ^ place, 0, keepdims=False) for place in range(4)],
        axis=1,
    )
    in_here = jnp.concatenate([in_own, swap(in_own)])
    exact = leaving.astype(F32)
    final_rows = (exact * gain_out).astype(BF16)
    final_squares = split_sum(jnp.sum(exact * exact, axis=1))
    partial_start = jnp.dot(final_rows, in_here, preferred_element_type=F32).astype(BF16)
    sent = jnp.concatenate([partial_start, final_squares], axis=1).reshape(32, 8, -1)
    got = lax.all_to_all(sent, "ty", 0, 0, tiled=True)
    (got,) = call(fold_kernel, [((16, sent.shape[2]), BF16)], got, name="fold")
    starts = with_others(got)
    depth_width = partial_start.shape[1]

    block_rows = got.shape[0]
    entries = codebook_table.shape[1]

    def by_core(value):
        return value.reshape(4, 2, 2, -1).transpose(1, 0, 2, 3).reshape(block_rows, -1)

    codes = lax.dynamic_slice_in_dim(codebook_ids, ty * block_rows, block_rows, 0)
    codes = by_core(codes) - tx * entries
    chosen = codes.T[: STEPS - 1, :, None] == jnp.arange(entries, dtype=jnp.int32)
    embeds = lax.dot_general(
        chosen.astype(BF16),
        codebook_table[: STEPS - 1],
        (((2,), (1,)), ((0,), (0,))),
        preferred_element_type=F32,
    ).astype(BF16)
    sides = jnp.split(embeds, 2, axis=2)
    sides = [side + flip(side, mask) for side, mask in zip(sides, (1, 3))]
    sides = [side + flip(side, mask) for side, mask in zip(sides, (3, 1))]
    owner_count = lax.axis_size("ty")
    block_owners = lax.dynamic_slice_in_dim(owners, ty * block_rows, block_rows, 0)
    same = block_owners[:, None] == block_owners[None, :]
    place = jnp.arange(block_rows)
    rank = jnp.sum((same & (place[None, :] < place[:, None])).astype(jnp.int32), axis=1)
    slots = by_core(block_owners * CAPACITY + rank)
    pre_gain = pre_gain.reshape(1, -1)
    head_gain = head_gain.reshape(1, -1)
    gate, up = load(mlp_gate, mlp_up, got)
    shape = (block_rows, depth_width)
    state, part, codes, slots, found, down = call(
        functools.partial(first_kernel, full_width),
        [
            (shape, F32),
            (shape, BF16),
            (codes.shape, jnp.int32),
            (slots.shape, jnp.int32),
            ((block_rows, 128), F32),
            pltpu.VMEM(mlp_down.shape, BF16),
        ],
        *starts,
        codes,
        slots,
        pre_gain,
        gate,
        up,
        in_hbm(mlp_down),
        name="depth_first",
        specs=[VMEM] * 9 + [HBM],
        scratch=[pltpu.SemaphoreType.DMA((4,))],
    )
    table_shape = codebook_table.shape[1:]
    for step in range(STEPS - 1):
        parts = with_others(part)
        state, part, outer = call(
            functools.partial(middle_kernel, step),
            [(shape, F32), (shape, BF16), (shape, BF16)],
            state,
            *parts,
            found,
            *sides,
            pre_gain,
            head_gain,
            gate,
            up,
            down,
            name="depth_step",
        )
        found, *extra = call(
            functools.partial(score_kernel if step else score_first_kernel, step),
            [(found.shape, F32)] + [pltpu.VMEM(table_shape, BF16)] * (step == 0),
            outer,
            codes,
            found,
            in_hbm(codebook_table),
            name="depth_score",
            specs=[VMEM] * 3 + [HBM],
            scratch=[pltpu.VMEM(table_shape, BF16), pltpu.SemaphoreType.DMA((2,))],
        )
        if step == 0:
            (last_table,) = extra
    parts = with_others(part)
    outgoing, other = call(
        functools.partial(last_kernel, STEPS - 1),
        [((owner_count, 4, 128), F32), (other.shape, BF16)],
        state,
        *parts,
        found,
        codes,
        slots,
        head_gain,
        last_table,
        other,
        name="depth_last",
    )

    incoming = lax.all_to_all(outgoing.reshape(devices, 128), ("ty", "tx"), 0, 0, tiled=True)
    other = other.reshape(devices, 1, 2, width)
    mine = leaving[:, :width].reshape(devices, 1, 2, width)
    hidden_out = jnp.where(
        core == 0,
        jnp.concatenate([mine, other], axis=1),
        jnp.concatenate([other, mine], axis=1),
    ).reshape(rows, width)
    incoming = jnp.sum(incoming.reshape(owner_count, 4, -1), axis=1)
    incoming = incoming[:, : 128 // 2].reshape(owner_count * CAPACITY, -1)
    logprob = incoming[:, STEPS : 2 * STEPS] - jnp.log(incoming[:, :STEPS])
    logprob = jnp.where(incoming[:, 2 * STEPS : 2 * STEPS + 1] > 0.0, logprob, 0.0)
    return (hidden_out, logprob.T[None])


def solution(mesh):
    placed = (
        P(None, ("ty", "tx")),
        P(("ty", "tx")),
        P("ty", "tx"),
        P(),
        P(("ty", "tx"), None, None),
        P(("ty", "tx"), None, None),
        P(("ty", "tx")),
        P("tx", "ty"),
        P(("ty", "tx")),
        P("ty", "tx"),
        P(),
        P(),
        P(None, "tx"),
        P(None, "tx"),
        P("tx", None),
        P(),
        P(),
        P(None, "tx", None),
    )
    return jax.shard_map(
        body,
        mesh=mesh,
        in_specs=placed,
        out_specs=(P(None, ("ty", "tx")), P("ty", None, None)),
        check_vma=False,
    )
```
